32 devices in a mesh: gx: 4 (over z), gy: 8 (over y, x, core).
Axes of the slice: x: 2, y: 2, z: 4, core: 2. Of those that a mesh axis runs over, the one named last changes fastest.
Arguments:
- positions: float32 [3, 65536], P(None, ('gx', 'gy')), may hold values from -1 to 1
- normals: float32 [3, 65536], P(None, ('gx', 'gy')), may hold values from -4 to 4
- emission: float32 [16, 65536], P(None, ('gx', 'gy')), may hold values from 0.05 to 2
- material: int32 [65536], P(('gx', 'gy')), may hold values from 0 to 7
- area_level: int32 [65536], P(('gx', 'gy')), may hold values from 0 to 7
- reflect_table: float32 [8, 16], replicated, may hold values from 0.1 to 0.9
- area_table: float32 [8], replicated, may hold values from 0.002 to 0.008
- pair_slots: int32 [32, 32, 2, 2], P(('gx', 'gy')), may hold values from -1 to 7, as said below
Outputs:
- radiosity: float32 [16, 65536], P(None, ('gx', 'gy'))
The draws below stay inside these ranges and needn't reach their ends.
Inputs may be any that keep to these rules, and one draw needn't show every extreme that they name: `pair_slots`: in slot [q, p, c], a row entry is -1 exactly when its column entry is -1; the non-empty slots of one [q, p] come first, at most 2 of them, and the slot group [q, q] is always full. No unordered pair of blocks occurs twice, and a slot never names the same block twice.
All inputs are finite; a program needn't handle non-finite values.
Results may differ from the reference program's by a relative error of at most 0.0017.
Values may be sent and summed in bfloat16 or wider, within the bound.
No kernel may reach another device: no remote copies, remote signals or barrier semaphores. Data moves between devices by JAX's collectives and lax.ppermute only.
A program may use at most 64 MiB of HBM per device.

```python
import math
import jax
import jax.numpy as jnp
from jax import lax

BANDS = 16
BLK = 256
BLOCKS_DEV = 8
CAP = 2
ITERS = 2
MATS = 8
LEVELS = 8
PATCHES = 65536
N_GX = 4
N_GY = 8


def draw_pair_slots(key, part):
    total_dev = N_GX * N_GY
    half = BLOCKS_DEV // 2
    key_count = jax.random.fold_in(key, 11)
    key_offset = jax.random.fold_in(key, 12)
    key_column = jax.random.fold_in(key, 13)
    owner = jnp.arange(total_dev, dtype=jnp.int32)[:, None]
    peer = jnp.arange(total_dev, dtype=jnp.int32)[None, :]
    counts = jax.random.randint(key_count, (total_dev, total_dev), 0, CAP + 1, dtype=jnp.int32)
    counts = jnp.where(owner == peer, CAP, counts)
    offset = jax.random.randint(key_offset, (total_dev, total_dev), 0, half, dtype=jnp.int32)
    slot_ids = jnp.arange(CAP, dtype=jnp.int32)
    row_low = (offset[:, :, None] + slot_ids[None, None, :]) % half
    col_low = jax.random.randint(key_column, (total_dev, total_dev, CAP), 0, half, dtype=jnp.int32)
    below = (owner < peer)[:, :, None]
    above = (owner > peer)[:, :, None]
    row_pick = jnp.where(above, row_low + half, row_low)
    col_pick = jnp.where(below, col_low, col_low + half)
    filled = slot_ids[None, None, :] < counts[:, :, None]
    row_pick = jnp.where(filled, row_pick, -1)
    col_pick = jnp.where(filled, col_pick, -1)
    return jnp.stack([row_pick, col_pick], axis=-1).astype(jnp.int32)


def place_ends(array, stream_key, low, top_value):
    spot = [jax.random.randint(jax.random.fold_in(stream_key, axis), (), 0, length) for axis, length in enumerate(array.shape)]
    main_axis = array.shape.index(max(array.shape))
    next_to = spot[:main_axis] + [(spot[main_axis] + 1) % array.shape[main_axis]] + spot[main_axis + 1:]
    return array.at[tuple(spot)].set(low).at[tuple(next_to)].set(top_value)


def steps_of(own_key, shape, split, low, high):
    def one(dim, shards_of):
        heights = jax.random.uniform(jax.random.fold_in(jax.random.fold_in(own_key, 6), dim), (shards_of,), jnp.float32, low / len(split), high / len(split))
        return jnp.repeat(jnp.exp(heights), shape[dim] // shards_of).reshape((-1,) + (1,) * (len(shape) - dim - 1))

    gain = one(*split[0])
    for cut in split[1:]:
        gain = gain * one(*cut)
    return gain


def normal_values(key, dims, scale, limit, split=(), kind=jnp.bfloat16):
    factor_of = steps_of(key, dims, split, -0.22, 0.18) if split else 1.0
    result = jax.random.normal(key, dims, jnp.float32) * scale * factor_of
    return jnp.minimum(jnp.maximum(result, -limit), limit).astype(kind)


def setup_inputs(seed: int = 0) -> dict:
    splits = jax.random.split(jax.random.key(seed), 9)
    positions = jnp.clip(jax.random.uniform(splits[0], (3, PATCHES), jnp.float32, -1.0, 1.0) * steps_of(splits[0], (3, PATCHES), ((1, 32),), -0.4, 0.0), -1.0, 1.0)
    normals = normal_values(splits[1], (3, PATCHES), 1.0, 4.0, ((1, 32),), jnp.float32)
    emission = jnp.clip(jnp.exp(math.log(2.0) - 3.6888794 * jax.random.uniform(splits[2], (BANDS, PATCHES), jnp.float32) ** steps_of(splits[2], (BANDS, PATCHES), ((1, 32),), -0.2, 0.2)), 0.05, 2.0)
    material = place_ends(jax.random.randint(splits[3], (PATCHES,), 0, MATS), jax.random.fold_in(splits[3], 1), 0, MATS - 1).astype(jnp.int32)
    area_level = place_ends(jax.random.randint(splits[4], (PATCHES,), 0, LEVELS), jax.random.fold_in(splits[4], 1), 0, LEVELS - 1).astype(jnp.int32)
    reflect_table = jnp.clip(jax.random.uniform(splits[5], (MATS, BANDS), jnp.float32, 0.1, 0.9), 0.1, 0.9)
    area_table = jnp.clip(jnp.exp(jax.random.uniform(splits[6], (LEVELS,), jnp.float32, math.log(0.002), math.log(0.008))), 0.002, 0.008)
    pair_slots = draw_pair_slots(jax.random.fold_in(splits[8], 71), 0)
    return dict(positions=positions, normals=normals, emission=emission, material=material, area_level=area_level, reflect_table=reflect_table, area_table=area_table, pair_slots=pair_slots)


def view_tile(row_geo, col_geo):
    delta = [col_geo[k][None, :] - row_geo[k][:, None] for k in range(3)]
    squared = delta[0] * delta[0] + delta[1] * delta[1] + delta[2] * delta[2]
    facing = jnp.maximum(row_geo[3][:, None] * delta[0] + row_geo[4][:, None] * delta[1] + row_geo[5][:, None] * delta[2], 0.0)
    seen = jnp.maximum(-(col_geo[3][None, :] * delta[0] + col_geo[4][None, :] * delta[1] + col_geo[5][None, :] * delta[2]), 0.0)
    mean_area = 0.5 * (row_geo[6][:, None] + col_geo[6][None, :])
    return facing * seen / ((squared + mean_area) * (math.pi * squared + mean_area))


def reference(positions, normals, emission, material, area_level, reflect_table, area_table, pair_slots):
    total_dev = N_GX * N_GY
    nblocks = PATCHES // BLK
    area = area_table[area_level]
    reflect = jnp.transpose(reflect_table)[:, material]
    geometry = jnp.concatenate([positions, normals, area[None, :]], axis=0)
    geo_blocks = jnp.transpose(geometry.reshape(7, nblocks, BLK), (1, 0, 2))
    owner = jnp.broadcast_to(jnp.arange(total_dev, dtype=jnp.int32)[:, None, None], (total_dev, total_dev, CAP))
    peer = jnp.broadcast_to(jnp.arange(total_dev, dtype=jnp.int32)[None, :, None], (total_dev, total_dev, CAP))
    row_local = pair_slots[..., 0]
    col_local = pair_slots[..., 1]
    usable = (row_local >= 0).astype(jnp.float32)
    row_block = (owner * BLOCKS_DEV + jnp.maximum(row_local, 0)).astype(jnp.int32).reshape(-1, 32)
    col_block = (peer * BLOCKS_DEV + jnp.maximum(col_local, 0)).astype(jnp.int32).reshape(-1, 32)
    usable = usable.reshape(-1, 32)
    radiosity = emission
    for sweep in range(ITERS):
        flux = (area[None, :] * radiosity).astype(jnp.bfloat16)
        flux_blocks = jnp.transpose(flux.reshape(BANDS, nblocks, BLK), (1, 0, 2))

        def one_group(carry, item):
            rows_here, cols_here, mask_here = item
            tiles = jax.vmap(view_tile)(geo_blocks[rows_here], geo_blocks[cols_here])
            tiles = (tiles * mask_here[:, None, None]).astype(jnp.bfloat16).astype(jnp.float32)
            own = jnp.einsum('sbj,sij->sbi', flux_blocks[cols_here].astype(jnp.float32), tiles)
            back = jnp.einsum('sbi,sij->sbj', flux_blocks[rows_here].astype(jnp.float32), tiles)
            carry = carry.at[rows_here].add(own)
            carry = carry.at[cols_here].add(back)
            return carry, None

        start = jnp.zeros((nblocks, BANDS, BLK), jnp.float32)
        summed, unused = lax.scan(one_group, start, (row_block, col_block, usable))
        irradiation = jnp.transpose(summed, (1, 0, 2)).reshape(BANDS, PATCHES)
        radiosity = emission + reflect * irradiation
    return radiosity
```

```python
import functools
import math

import jax
import jax.numpy as jnp
from jax import lax
from jax.experimental import pallas as pl
from jax.experimental.pallas import tpu as pltpu
from jax.sharding import PartitionSpec as P

BANDS = 16
BLK = 256
CAP = 2
GEO = 16
KDIM = 48
KEEP_BYTES = 24 * 2**20
BF16 = jnp.bfloat16
F32 = jnp.float32

VMEM = functools.partial(pl.BlockSpec, memory_space=pltpu.VMEM)
SMEM = functools.partial(pl.BlockSpec, memory_space=pltpu.SMEM)


def split(value, terms):
    out = []
    for _ in range(terms):
        part = value.astype(BF16).astype(F32)
        out.append(part)
        value = value - part
    return out


def pack_kernel(pos_ref, nrm_ref, emi_ref, level_ref, table_ref, slot_ref, pay_ref, geo_ref, area_ref, rows):
    level = level_ref[...]
    area = jnp.zeros(level.shape, F32)
    for k in range(table_ref.shape[0]):
        area = jnp.where(level == k, table_ref[k], area)
    area_ref[...] = area
    p1, p2 = split(pos_ref[...], 2)
    n1, n2 = split(nrm_ref[...], 2)
    a1, a2 = split(area, 2)
    rows[0:3, :] = p1
    rows[3:6, :] = p2
    rows[6:9, :] = n1
    rows[9:12, :] = n2
    rows[12:13, :] = a1
    rows[13:14, :] = a2
    rows[14:15, :] = slot_ref[...]
    rows[15:16, :] = jnp.zeros_like(area)
    geo = rows[...].astype(BF16)
    geo_ref[...] = geo
    pay_ref[0:GEO, :] = geo
    pay_ref[GEO:, :] = (area * emi_ref[...]).astype(BF16)


def constants(g):
    p = g[0:3] + g[3:6]
    n = g[6:9] + g[9:12]
    half = 0.5 * (g[12:13] + g[13:14])
    pp = p[0:1] * p[0:1] + p[1:2] * p[1:2] + p[2:3] * p[2:3]
    np_ = n[0:1] * p[0:1] + n[1:2] * p[1:2] + n[2:3] * p[2:3]
    return p, split(pp + half, 3), split(math.pi * pp + half, 3), split(-np_, 3)


def column_features(g, feat):
    _, q, r, c = constants(g)
    one = jnp.ones_like(q[0])
    feat[0:12, :] = g[0:12]
    feat[12:24, :] = g[0:12]
    feat[24:30, :] = g[0:6]
    for t in range(3):
        feat[30 + t : 31 + t, :] = q[t]
        feat[33 + t : 34 + t, :] = r[t]
        feat[36 + t : 37 + t, :] = c[t]
        feat[39 + t : 40 + t, :] = one
    feat[42:48, :] = jnp.zeros((6,) + one.shape[1:], F32)


def row_features(g, feat, variant):
    p, q, r, c = constants(g)
    one = jnp.ones_like(q[0])
    feat[...] = jnp.zeros(feat.shape, F32)
    if variant == 0:
        feat[0:3, :] = g[6:9]
        feat[3:6, :] = g[6:9]
        feat[12:15, :] = g[9:12]
        feat[15:18, :] = g[9:12]
        last = c
    elif variant == 1:
        feat[6:9, :] = g[0:3]
        feat[9:12, :] = g[0:3]
        feat[18:21, :] = g[3:6]
        feat[21:24, :] = g[3:6]
        for t in range(3):
            feat[36 + t : 37 + t, :] = one
        last = None
    elif variant == 2:
        u1, u2 = -2.0 * g[0:3], -2.0 * g[3:6]
        feat[0:3, :] = u1
        feat[3:6, :] = u1
        feat[12:15, :] = u2
        feat[15:18, :] = u2
        for t in range(3):
            feat[30 + t : 31 + t, :] = one
        last = q
    else:
        u1, u2, u3 = split((-2.0 * math.pi) * p, 3)
        feat[0:3, :] = u1
        feat[3:6, :] = u1
        feat[12:15, :] = u2
        feat[15:18, :] = u2
        feat[24:27, :] = u3
        feat[27:30, :] = u3
        for t in range(3):
            feat[33 + t : 34 + t, :] = one
        last = r
    if last is not None:
        for t in range(3):
            feat[39 + t : 40 + t, :] = last[t]


def list_pairs(nz, ny, nb, place_ref, slots, pairs):
    z, k = place_ref[0], place_ref[1]
    most = nz * ny * 2 * CAP

    def peer(e, count):
        s = e // ny
        m = e % ny
        zs = lax.rem(z - s + nz, nz)
        own = (z * ny + jnp.bitwise_xor(k, m)) * (2 * CAP)
        served = (zs * ny + k) * (2 * CAP)
        for t in range(CAP):
            row, col = slots[s, own + 2 * t], slots[s, own + 2 * t + 1]
            pairs[count] = (s * nb + row) * 4096 + m * nb + col
            count = count + (row >= 0).astype(jnp.int32)
            col, row = slots[nz + m, served + 2 * t], slots[nz + m, served + 2 * t + 1]
            pairs[count] = (s * nb + row) * 4096 + m * nb + col
            count = count + (row >= 0).astype(jnp.int32)
        return count

    pairs[most + 1] = lax.fori_loop(0, nz * ny, peer, jnp.int32(0))


def put_out(nz, nb, acc, out_refs):
    for s in range(nz):
        for b in range(nb):
            out_refs[s][:, b * BLK : (b + 1) * BLK] = acc[s * nb + b].astype(out_refs[s].dtype)


def form_kernel(nz, ny, nb, keep, fresh, place_ref, *refs):
    geos, refs = refs[:nz], refs[nz:]
    pays, refs = refs[:ny], refs[ny:]
    if fresh:
        fluxes, refs = refs[:ny], refs[ny:]
    outs, refs = refs[:nz], refs[nz:]
    if keep:
        tiles_ref, pairs, refs = refs[0], refs[1], refs[2:]
    feat, row_feat, col_feat, flux, acc, slots_v, slots, sem, *more = refs
    if not keep:
        pairs = more[0]
    most = nz * ny * 2 * CAP
    width = slots.shape[1]
    for s in range(nz):
        g = geos[s][...].astype(F32)
        slots_v[s : s + 1, :] = g[14:15, :width].astype(jnp.int32)
    for m in range(ny):
        g = pays[m][0:GEO, :].astype(F32)
        slots_v[nz + m : nz + m + 1, :] = g[14:15, :width].astype(jnp.int32)
    copy = pltpu.make_async_copy(slots_v, slots, sem)
    copy.start()
    for s in range(nz):
        g = geos[s][...].astype(F32)
        for v in range(4):
            row_features(g, feat, v)
            for b in range(nb):
                row_feat[s * nb + b, v] = feat[:, b * BLK : (b + 1) * BLK].astype(BF16)
    for m in range(ny):
        g = pays[m][0:GEO, :].astype(F32)
        column_features(g, feat)
        for b in range(nb):
            col_feat[m * nb + b] = jnp.transpose(feat[:, b * BLK : (b + 1) * BLK]).astype(BF16)
            here = slice(b * BLK, (b + 1) * BLK)
            flux[m * nb + b] = fluxes[m][:, here] if fresh else pays[m][GEO:, here]
    acc[...] = jnp.zeros(acc.shape, F32)
    copy.wait()
    list_pairs(nz, ny, nb, place_ref, slots, pairs)

    def one(t, carry):
        code = pairs[t]
        rb = code // 4096
        cb = code % 4096
        parts = []
        for j in range(0, BLK, 64):
            left = col_feat[cb, j : j + 64, :]
            f, s, q, r = (
                jnp.dot(left, row_feat[rb, v], preferred_element_type=F32) for v in range(4)
            )
            top = jnp.maximum(f, 0.0) * jnp.maximum(s, 0.0)
            parts.append((top * pl.reciprocal(q * r, approx=True)).astype(BF16))
        tile = jnp.concatenate(parts, axis=0)
        if keep:
            tiles_ref[t] = tile
        acc[rb] += jnp.dot(flux[cb], tile, preferred_element_type=F32)
        return carry

    lax.fori_loop(0, pairs[most + 1], one, 0)
    put_out(nz, nb, acc, outs)


def apply_kernel(nz, ny, nb, pairs, tiles_ref, *refs):
    fluxes, refs = refs[:ny], refs[ny:]
    outs, refs = refs[:nz], refs[nz:]
    flux, acc = refs
    most = nz * ny * 2 * CAP
    for m in range(ny):
        for b in range(nb):
            flux[m * nb + b] = fluxes[m][:, b * BLK : (b + 1) * BLK]
    acc[...] = jnp.zeros(acc.shape, F32)

    def one(t, carry):
        code = pairs[t]
        rb = code // 4096
        cb = code % 4096
        acc[rb] += jnp.dot(flux[cb], tiles_ref[t], preferred_element_type=F32)
        return carry

    lax.fori_loop(0, pairs[most + 1], one, 0)
    put_out(nz, nb, acc, outs)


def per_device(nz, ny, positions, normals, emission, material, area_level, reflect_table, area_table, pair_slots):
    patches = positions.shape[1]
    nb = patches // BLK
    most = nz * ny * 2 * CAP
    width = most if nz * ny * 2 * CAP == pair_slots.size else pair_slots.size
    keep = most * BLK * BLK * 2 <= KEEP_BYTES
    params = pltpu.CompilerParams(vmem_limit_bytes=(30 if keep else 56) * 2**20)
    place = jnp.stack([lax.axis_index("gx"), lax.axis_index("gy")]).astype(jnp.int32)
    slot_row = pair_slots.reshape(1, -1).astype(F32)
    slot_row = jnp.pad(slot_row, ((0, 0), (0, patches - slot_row.shape[1])))
    payload, geo, area = pl.pallas_call(
        pack_kernel,
        out_shape=(
            jax.ShapeDtypeStruct((GEO + BANDS, patches), BF16),
            jax.ShapeDtypeStruct((GEO, patches), BF16),
            jax.ShapeDtypeStruct((1, patches), F32),
        ),
        in_specs=[VMEM()] * 4 + [SMEM(), VMEM()],
        out_specs=(VMEM(),) * 3,
        scratch_shapes=[pltpu.VMEM((GEO, patches), F32)],
        name="pack",
    )(positions, normals, emission, area_level.reshape(1, patches), area_table, slot_row)

    def along(x):
        return [lax.ppermute(x, "gx", [(i, (i + s) % nz) for i in range(nz)]) for s in range(1, nz)]

    def plane(x):
        got = {0: x}
        for m in range(2, ny, 2):
            got[m] = lax.ppermute(x, "gy", [(i, i ^ m) for i in range(ny)])
        for m in range(0, ny, 2):
            got[m + 1] = lax.ppermute(got[m], "gy", [(i, i ^ 1) for i in range(ny)])
        return [got[m] for m in range(ny)]

    def home(parts):
        total = parts[0]
        for s in range(1, nz):
            back = lax.ppermute(parts[s], "gx", [(i, (i - s) % nz) for i in range(nz)])
            total = total + back.astype(F32)
        return total

    rows = [geo] + along(geo)
    cols = plane(payload)
    out_parts = [jax.ShapeDtypeStruct((BANDS, patches), F32)] + [
        jax.ShapeDtypeStruct((BANDS, patches), BF16)
    ] * (nz - 1)

    def form(fluxes):
        fresh = fluxes is not None
        outs = list(out_parts)
        specs = [VMEM()] * nz
        if keep:
            outs += [
                pltpu.VMEM((most, BLK, BLK), BF16),
                jax.ShapeDtypeStruct((most + 8,), jnp.int32),
            ]
            specs += [VMEM(), SMEM()]
        scratch = [
            pltpu.VMEM((KDIM, patches), F32),
            pltpu.VMEM((nz * nb, 4, KDIM, BLK), BF16),
            pltpu.VMEM((ny * nb, BLK, KDIM), BF16),
            pltpu.VMEM((ny * nb, BANDS, BLK), BF16),
            pltpu.VMEM((nz * nb, BANDS, BLK), F32),
            pltpu.VMEM((-(-(nz + ny) // 8) * 8, width), jnp.int32),
            pltpu.SMEM((-(-(nz + ny) // 8) * 8, width), jnp.int32),
            pltpu.SemaphoreType.DMA,
        ]
        if not keep:
            scratch += [pltpu.SMEM((most + 8,), jnp.int32)]
        return pl.pallas_call(
            functools.partial(form_kernel, nz, ny, nb, keep, fresh),
            out_shape=tuple(outs),
            in_specs=[SMEM()] + [VMEM()] * (nz + ny + (ny if fresh else 0)),
            out_specs=tuple(specs),
            scratch_shapes=scratch,
            compiler_params=params,
            name="form",
        )(place, *rows, *cols, *(fluxes or []))

    def apply(pairs, tiles, fluxes):
        return pl.pallas_call(
            functools.partial(apply_kernel, nz, ny, nb),
            out_shape=tuple(out_parts),
            in_specs=[SMEM()] + [VMEM()] * (1 + ny),
            out_specs=(VMEM(),) * nz,
            scratch_shapes=[
                pltpu.VMEM((ny * nb, BANDS, BLK), BF16),
                pltpu.VMEM((nz * nb, BANDS, BLK), F32),
            ],
            compiler_params=params,
            name="apply",
        )(pairs, tiles, *fluxes)

    kind_hot = (
        material[None, :] == jnp.arange(reflect_table.shape[0], dtype=jnp.int32)[:, None]
    ).astype(F32)
    reflect = jnp.dot(jnp.transpose(reflect_table), kind_hot, precision=lax.Precision.HIGHEST)

    first = form(None)
    radiosity = emission + reflect * home(first[:nz])
    fluxes = plane((area * radiosity).astype(BF16))
    second = apply(first[nz + 1], first[nz], fluxes) if keep else form(fluxes)
    return emission + reflect * home(second[:nz])


def solution(mesh):
    nz, ny = mesh.shape["gx"], mesh.shape["gy"]
    both = ("gx", "gy")
    placed = (
        P(None, both),
        P(None, both),
        P(None, both),
        P(both),
        P(both),
        P(),
        P(),
        P(both, None, None, None),
    )
    return jax.shard_map(
        functools.partial(per_device, nz, ny),
        mesh=mesh,
        in_specs=placed,
        out_specs=P(None, both),
        check_vma=False,
    )
```

```python
import functools
import math

import jax
import jax.numpy as jnp
from jax import lax
from jax.experimental import pallas as pl
from jax.experimental.pallas import tpu as pltpu
from jax.sharding import PartitionSpec as P

BANDS = 16
BLK = 256
CAP = 2
GEO = 16
LANES = 128
KDIM = 48
FORM_UNROLL = 4
APPLY_UNROLL = 8
SPARE = 8
KEEP_BYTES = 24 * 2**20
BF16 = jnp.bfloat16
F32 = jnp.float32

VMEM = functools.partial(pl.BlockSpec, memory_space=pltpu.VMEM)
SMEM = functools.partial(pl.BlockSpec, memory_space=pltpu.SMEM)


def split(value, terms):
    out = []
    for _ in range(terms):
        part = value.astype(BF16).astype(F32)
        out.append(part)
        value = value - part
    return out


def pack_kernel(pos_ref, nrm_ref, emi_ref, level_ref, table_ref, slot_ref, pay_ref, geo_ref, area_ref, rows):
    level = level_ref[...]
    area = jnp.zeros(level.shape, F32)
    for k in range(table_ref.shape[0]):
        area = jnp.where(level == k, table_ref[k], area)
    area_ref[...] = area
    p1, p2 = split(pos_ref[...], 2)
    n1, n2 = split(nrm_ref[...], 2)
    a1, a2 = split(area, 2)
    rows[0:3, :] = p1
    rows[3:6, :] = p2
    rows[6:9, :] = n1
    rows[9:12, :] = n2
    rows[12:13, :] = a1
    rows[13:14, :] = a2
    rows[14:16, :] = jnp.zeros((2, area.shape[1]), F32)
    peers = slot_ref.shape[-1]
    for t in range(2 * CAP):
        rows[14:15, t * LANES : t * LANES + peers] = slot_ref[t // 2, t % 2 : t % 2 + 1, :].astype(F32)
    geo = rows[...].astype(BF16)
    geo_ref[...] = geo
    pay_ref[0:GEO, :] = geo
    pay_ref[GEO:, :] = (area * emi_ref[...]).astype(BF16)


def constants(g):
    p = g[0:3] + g[3:6]
    n = g[6:9] + g[9:12]
    half = 0.5 * (g[12:13] + g[13:14])
    pp = p[0:1] * p[0:1] + p[1:2] * p[1:2] + p[2:3] * p[2:3]
    np_ = n[0:1] * p[0:1] + n[1:2] * p[1:2] + n[2:3] * p[2:3]
    return p, split(pp + half, 3), split(math.pi * pp + half, 3), split(-np_, 3)


def column_features(g, feat):
    _, q, r, c = constants(g)
    one = jnp.ones_like(q[0])
    feat[0:12, :] = g[0:12]
    feat[12:24, :] = g[0:12]
    feat[24:30, :] = g[0:6]
    for t in range(3):
        feat[30 + t : 31 + t, :] = q[t]
        feat[33 + t : 34 + t, :] = r[t]
        feat[36 + t : 37 + t, :] = c[t]
        feat[39 + t : 40 + t, :] = one
    feat[42:48, :] = jnp.zeros((6,) + one.shape[1:], F32)


def row_features(g, feat, variant):
    p, q, r, c = constants(g)
    one = jnp.ones_like(q[0])
    feat[...] = jnp.zeros(feat.shape, F32)
    if variant == 0:
        feat[0:3, :] = g[6:9]
        feat[3:6, :] = g[6:9]
        feat[12:15, :] = g[9:12]
        feat[15:18, :] = g[9:12]
        last = c
    elif variant == 1:
        feat[6:9, :] = g[0:3]
        feat[9:12, :] = g[0:3]
        feat[18:21, :] = g[3:6]
        feat[21:24, :] = g[3:6]
        for t in range(3):
            feat[36 + t : 37 + t, :] = one
        last = None
    elif variant == 2:
        u1, u2 = -2.0 * g[0:3], -2.0 * g[3:6]
        feat[0:3, :] = u1
        feat[3:6, :] = u1
        feat[12:15, :] = u2
        feat[15:18, :] = u2
        for t in range(3):
            feat[30 + t : 31 + t, :] = one
        last = q
    else:
        u1, u2, u3 = split((-2.0 * math.pi) * p, 3)
        feat[0:3, :] = u1
        feat[3:6, :] = u1
        feat[12:15, :] = u2
        feat[15:18, :] = u2
        feat[24:27, :] = u3
        feat[27:30, :] = u3
        for t in range(3):
            feat[33 + t : 34 + t, :] = one
        last = r
    if last is not None:
        for t in range(3):
            feat[39 + t : 40 + t, :] = last[t]


def list_pairs(nz, ny, nb, place_ref, slots, pairs):
    z, k = place_ref[0], place_ref[1]
    most = nz * ny * 2 * CAP

    def peer(e, count):
        s = e // ny
        m = e % ny
        zs = lax.rem(z - s + nz, nz)
        own = z * ny + jnp.bitwise_xor(k, m)
        served = zs * ny + k
        for t in range(CAP):
            row, col = slots[s, 2 * t * LANES + own], slots[s, (2 * t + 1) * LANES + own]
            pairs[count] = (s * nb + row) * 4096 + m * nb + col
            count = count + (row >= 0).astype(jnp.int32)
            col, row = slots[nz + m, 2 * t * LANES + served], slots[nz + m, (2 * t + 1) * LANES + served]
            pairs[count] = (s * nb + row) * 4096 + m * nb + col
            count = count + (row >= 0).astype(jnp.int32)
        return count

    count = lax.fori_loop(0, nz * ny, peer, jnp.int32(0))
    for t in range(SPARE):
        pairs[count + t] = nz * nb * 4096
    pairs[most + SPARE] = count


def put_out(nz, nb, acc, out_refs):
    for s in range(nz):
        for b in range(nb):
            out_refs[s][:, b * BLK : (b + 1) * BLK] = acc[s * nb + b].astype(out_refs[s].dtype)


def form_kernel(nz, ny, nb, keep, fresh, place_ref, *refs):
    geos, refs = refs[:nz], refs[nz:]
    pays, refs = refs[:ny], refs[ny:]
    if fresh:
        fluxes, refs = refs[:ny], refs[ny:]
    outs, refs = refs[:nz], refs[nz:]
    if keep:
        tiles_ref, pairs, refs = refs[0], refs[1], refs[2:]
    feat, row_feat, col_feat, flux, acc, slots_v, slots, sem, *more = refs
    if not keep:
        pairs = more[0]
    most = nz * ny * 2 * CAP
    width = slots.shape[1]
    for s in range(nz):
        g = geos[s][...].astype(F32)
        slots_v[s : s + 1, :] = g[14:15, :width].astype(jnp.int32)
    for m in range(ny):
        g = pays[m][0:GEO, :].astype(F32)
        slots_v[nz + m : nz + m + 1, :] = g[14:15, :width].astype(jnp.int32)
    copy = pltpu.make_async_copy(slots_v, slots, sem)
    copy.start()
    for s in range(nz):
        g = geos[s][...].astype(F32)
        for v in range(4):
            row_features(g, feat, v)
            for b in range(nb):
                row_feat[s * nb + b, v] = feat[:, b * BLK : (b + 1) * BLK].astype(BF16)
    for m in range(ny):
        g = pays[m][0:GEO, :].astype(F32)
        column_features(g, feat)
        for b in range(nb):
            col_feat[m * nb + b] = jnp.transpose(feat[:, b * BLK : (b + 1) * BLK]).astype(BF16)
            here = slice(b * BLK, (b + 1) * BLK)
            flux[m * nb + b] = fluxes[m][:, here] if fresh else pays[m][GEO:, here]
    acc[...] = jnp.zeros(acc.shape, F32)
    copy.wait()
    list_pairs(nz, ny, nb, place_ref, slots, pairs)

    count = pairs[most + SPARE]

    def tile_of(t):
        code = pairs[t]
        rb = jnp.minimum(code // 4096, nz * nb - 1)
        left = col_feat[code % 4096]
        f, s, q, r = (
            jnp.dot(left, row_feat[rb, v], preferred_element_type=F32) for v in range(4)
        )
        top = jnp.maximum(f, 0.0) * jnp.maximum(s, 0.0)
        return (top * pltpu.reciprocal(q * r, approx=True)).astype(BF16)

    if keep:

        def some(t, carry):
            for u in range(FORM_UNROLL):
                tiles_ref[t * FORM_UNROLL + u] = tile_of(t * FORM_UNROLL + u)
            return carry

        lax.fori_loop(0, (count + FORM_UNROLL - 1) // FORM_UNROLL, some, 0)
        apply_tiles(count, pairs, tiles_ref, flux, acc)
    else:

        def one(t, carry):
            code = pairs[t]
            acc[code // 4096] += jnp.dot(flux[code % 4096], tile_of(t), preferred_element_type=F32)
            return carry

        lax.fori_loop(0, count, one, 0)
    put_out(nz, nb, acc, outs)


def apply_tiles(count, pairs, tiles_ref, flux, acc):
    def some(t, carry):
        sums = []
        for u in range(APPLY_UNROLL):
            code = pairs[t * APPLY_UNROLL + u]
            tile = tiles_ref[t * APPLY_UNROLL + u]
            sums.append((code // 4096, jnp.dot(flux[code % 4096], tile, preferred_element_type=F32)))
        for rb, total in sums:
            acc[rb] += total
        return carry

    lax.fori_loop(0, (count + APPLY_UNROLL - 1) // APPLY_UNROLL, some, 0)


def apply_kernel(nz, ny, nb, pairs, tiles_ref, *refs):
    fluxes, refs = refs[:ny], refs[ny:]
    outs, refs = refs[:nz], refs[nz:]
    flux, acc = refs
    most = nz * ny * 2 * CAP
    for m in range(ny):
        for b in range(nb):
            flux[m * nb + b] = fluxes[m][:, b * BLK : (b + 1) * BLK]
    acc[...] = jnp.zeros(acc.shape, F32)
    apply_tiles(pairs[most + SPARE], pairs, tiles_ref, flux, acc)
    put_out(nz, nb, acc, outs)


def per_device(nz, ny, positions, normals, emission, material, area_level, reflect_table, area_table, pair_slots):
    patches = positions.shape[1]
    nb = patches // BLK
    most = nz * ny * 2 * CAP
    width = 2 * CAP * LANES
    keep = (most + SPARE) * BLK * BLK * 2 <= KEEP_BYTES
    params = [pltpu.CompilerParams(vmem_limit_bytes=n * 2**20) for n in ((14, 4) if keep else (56, 4))]
    place = jnp.stack([lax.axis_index("gx"), lax.axis_index("gy")]).astype(jnp.int32)
    slot_rows = jnp.transpose(pair_slots[0], (1, 2, 0))
    payload, geo, area = pl.pallas_call(
        pack_kernel,
        out_shape=(
            pltpu.VMEM((GEO + BANDS, patches), BF16),
            pltpu.VMEM((GEO, patches), BF16),
            jax.ShapeDtypeStruct((1, patches), F32),
        ),
        in_specs=[VMEM()] * 4 + [SMEM(), VMEM()],
        out_specs=(VMEM(),) * 3,
        scratch_shapes=[pltpu.VMEM((GEO, patches), F32)],
        name="pack",
    )(positions, normals, emission, area_level.reshape(1, patches), area_table, slot_rows)

    def along(x):
        return [lax.ppermute(x, "gx", [(i, (i + s) % nz) for i in range(nz)]) for s in range(1, nz)]

    def plane(x):
        got = {0: x}
        for m in range(2, ny, 2):
            got[m] = lax.ppermute(x, "gy", [(i, i ^ m) for i in range(ny)])
        for m in range(0, ny, 2):
            got[m + 1] = lax.ppermute(got[m], "gy", [(i, i ^ 1) for i in range(ny)])
        return [got[m] for m in range(ny)]

    def home(parts):
        total = parts[0]
        for s in range(1, nz):
            back = lax.ppermute(parts[s], "gx", [(i, (i - s) % nz) for i in range(nz)])
            total = total + back.astype(F32)
        return total

    rows = [geo] + along(geo)
    cols = plane(payload)
    out_parts = [jax.ShapeDtypeStruct((BANDS, patches), F32)] + [
        jax.ShapeDtypeStruct((BANDS, patches), BF16)
    ] * (nz - 1)

    def form(fluxes):
        fresh = fluxes is not None
        outs = list(out_parts)
        specs = [VMEM()] * nz
        if keep:
            outs += [
                pltpu.VMEM((most + SPARE, BLK, BLK), BF16),
                jax.ShapeDtypeStruct((most + SPARE + 1,), jnp.int32),
            ]
            specs += [VMEM(), SMEM()]
        scratch = [
            pltpu.VMEM((KDIM, patches), F32),
            pltpu.VMEM((nz * nb, 4, KDIM, BLK), BF16),
            pltpu.VMEM((ny * nb, BLK, KDIM), BF16),
            pltpu.VMEM((ny * nb, BANDS, BLK), BF16),
            pltpu.VMEM((nz * nb + 1, BANDS, BLK), F32),
            pltpu.VMEM((-(-(nz + ny) // 8) * 8, width), jnp.int32),
            pltpu.SMEM((-(-(nz + ny) // 8) * 8, width), jnp.int32),
            pltpu.SemaphoreType.DMA,
        ]
        if not keep:
            scratch += [pltpu.SMEM((most + SPARE + 1,), jnp.int32)]
        return pl.pallas_call(
            functools.partial(form_kernel, nz, ny, nb, keep, fresh),
            out_shape=tuple(outs),
            in_specs=[SMEM()] + [VMEM()] * (nz + ny + (ny if fresh else 0)),
            out_specs=tuple(specs),
            scratch_shapes=scratch,
            compiler_params=params[0],
            name="form",
        )(place, *rows, *cols, *(fluxes or []))

    def apply(pairs, tiles, fluxes):
        return pl.pallas_call(
            functools.partial(apply_kernel, nz, ny, nb),
            out_shape=tuple(out_parts),
            in_specs=[SMEM()] + [VMEM()] * (1 + ny),
            out_specs=(VMEM(),) * nz,
            scratch_shapes=[
                pltpu.VMEM((ny * nb, BANDS, BLK), BF16),
                pltpu.VMEM((nz * nb + 1, BANDS, BLK), F32),
            ],
            compiler_params=params[1],
            name="apply",
        )(pairs, tiles, *fluxes)

    kind_hot = (
        material[None, :] == jnp.arange(reflect_table.shape[0], dtype=jnp.int32)[:, None]
    ).astype(F32)
    reflect = jnp.dot(jnp.transpose(reflect_table), kind_hot, precision=lax.Precision.HIGHEST)

    first = form(None)
    radiosity = emission + reflect * home(first[:nz])
    fluxes = plane((area * radiosity).astype(BF16))
    second = apply(first[nz + 1], first[nz], fluxes) if keep else form(fluxes)
    return emission + reflect * home(second[:nz])


def solution(mesh):
    nz, ny = mesh.shape["gx"], mesh.shape["gy"]
    both = ("gx", "gy")
    placed = (
        P(None, both),
        P(None, both),
        P(None, both),
        P(both),
        P(both),
        P(),
        P(),
        P(both, None, None, None),
    )
    return jax.shard_map(
        functools.partial(per_device, nz, ny),
        mesh=mesh,
        in_specs=placed,
        out_specs=P(None, both),
        check_vma=False,
    )
```

```python
import functools
import math

import jax
import jax.numpy as jnp
from jax import lax
from jax.experimental import pallas as pl
from jax.experimental.pallas import tpu as pltpu
from jax.sharding import PartitionSpec as P

BANDS = 16
BLK = 256
CAP = 2
GEO = 16
LANES = 128
KDIM = 48
FORM_UNROLL = 8
APPLY_UNROLL = 8
SPARE = 8
KEEP_BYTES = 24 * 2**20
BF16 = jnp.bfloat16
F32 = jnp.float32

VMEM = functools.partial(pl.BlockSpec, memory_space=pltpu.VMEM)
SMEM = functools.partial(pl.BlockSpec, memory_space=pltpu.SMEM)


def split(value, terms):
    out = []
    for _ in range(terms):
        part = value.astype(BF16).astype(F32)
        out.append(part)
        value = value - part
    return out


def pack_kernel(pos_ref, nrm_ref, emi_ref, level_ref, table_ref, slot_ref, pay_ref, geo_ref, area_ref, rows):
    level = level_ref[...]
    area = jnp.zeros(level.shape, F32)
    for k in range(table_ref.shape[0]):
        area = jnp.where(level == k, table_ref[k], area)
    area_ref[...] = area
    p1, p2 = split(pos_ref[...], 2)
    n1, n2 = split(nrm_ref[...], 2)
    a1, a2 = split(area, 2)
    rows[0:3, :] = p1
    rows[3:6, :] = p2
    rows[6:7, :] = a1
    rows[7:8, :] = a2
    rows[8:11, :] = n1
    rows[11:14, :] = n2
    rows[14:16, :] = jnp.zeros((2, area.shape[1]), F32)
    peers = slot_ref.shape[-1]
    for t in range(2 * CAP):
        rows[14:15, t * LANES : t * LANES + peers] = slot_ref[t // 2, t % 2 : t % 2 + 1, :].astype(F32)
    geo = rows[...].astype(BF16)
    geo_ref[...] = geo
    pay_ref[0:GEO, :] = geo
    pay_ref[GEO:, :] = (area * emi_ref[...]).astype(BF16)


def terms_of(g):
    pos, nrm = g[0:8], g[8:16]
    row = lax.broadcasted_iota(jnp.int32, pos.shape, 0)
    p = pos + pltpu.roll(pos, 5, 0)
    n = nrm + pltpu.roll(nrm, 5, 0)
    half = 0.5 * (pos[6:7] + pos[7:8])
    pp = jnp.sum(jnp.where(row < 3, p * p, 0.0), axis=0, keepdims=True)
    dot = jnp.sum(jnp.where(row < 3, n * p, 0.0), axis=0, keepdims=True)
    return pos, nrm, row, split(pp + half, 3), split(-dot, 3), (math.pi - 1.0) * half


def column_features(g):
    pos, nrm, row, q, c, h = terms_of(g)
    zero = jnp.zeros(pos.shape, F32)
    one = jnp.where(row == 6, 1.0, zero)
    pos = jnp.where(row < 6, pos, one)
    nrm = jnp.where(row < 6, nrm, one)
    consts, areas = zero, zero
    for t, value in enumerate(q + c):
        consts = jnp.where(row == t, value, consts)
    for t, value in enumerate(split(h, 3)):
        areas = jnp.where(row == t, value, areas)
    return jnp.concatenate([pos, nrm, pos, nrm, consts, areas], axis=0)


def row_features(g):
    pos, nrm, row, q, c, h = terms_of(g)
    zero = jnp.zeros(pos.shape, F32)

    def both(x):
        high = jnp.where(row < 3, x, pltpu.roll(x, 3, 0))
        low = jnp.where(row < 3, pltpu.roll(x, 5, 0), x)
        return jnp.where(row < 6, high, 0.0), jnp.where(row < 6, low, 0.0)

    def with_last(x, value):
        return jnp.where(row == 6, value, x)

    p_hi, p_lo = both(pos)
    n_hi, n_lo = both(nrm)
    facing = [with_last(n_hi, c[0]), with_last(zero, c[1]), with_last(n_lo, c[2]), zero, zero, zero]
    seen = [zero, p_hi, zero, p_lo, jnp.where((row >= 3) & (row < 6), 1.0, zero), zero]
    near = [
        with_last(-2.0 * p_hi, q[0]),
        with_last(zero, q[1]),
        with_last(-2.0 * p_lo, q[2]),
        zero,
        jnp.where(row < 3, 1.0, zero),
        zero,
    ]
    return [jnp.concatenate(parts, axis=0).astype(BF16) for parts in (facing, seen, near)], h


def list_pairs(nz, ny, nb, place_ref, slots, pairs):
    z, k = place_ref[0], place_ref[1]
    most = nz * ny * 2 * CAP

    def peer(e, count):
        s = e // ny
        m = e % ny
        zs = lax.rem(z - s + nz, nz)
        own = z * ny + jnp.bitwise_xor(k, m)
        served = zs * ny + k
        for t in range(CAP):
            row, col = slots[s, 2 * t * LANES + own], slots[s, (2 * t + 1) * LANES + own]
            pairs[count] = (s * nb + row) * 4096 + m * nb + col
            count = count + (row >= 0).astype(jnp.int32)
            col, row = slots[nz + m, 2 * t * LANES + served], slots[nz + m, (2 * t + 1) * LANES + served]
            pairs[count] = (s * nb + row) * 4096 + m * nb + col
            count = count + (row >= 0).astype(jnp.int32)
        return count

    count = jnp.int32(0)
    if nz * ny <= 32:
        for e in range(nz * ny):
            count = peer(e, count)
    else:
        count = lax.fori_loop(0, nz * ny, peer, count)
    for t in range(SPARE):
        pairs[count + t] = nz * nb * 4096
    pairs[most + SPARE] = count


def form_scratch(nz, ny, nb, patches):
    devices = -(-(nz + ny) // 8) * 8
    return [
        pltpu.VMEM((nz * nb, 3, KDIM, BLK), BF16),
        pltpu.VMEM((nz * nb, 1, BLK), F32),
        pltpu.VMEM((ny * nb, BLK, KDIM), BF16),
        pltpu.VMEM((ny * nb, BLK, LANES), F32),
        pltpu.VMEM((ny * nb, BANDS, BLK), BF16),
        pltpu.VMEM((nz * nb + 1, BANDS, BLK), F32),
        pltpu.VMEM((devices, 2 * CAP * LANES), jnp.int32),
        pltpu.SMEM((devices, 2 * CAP * LANES), jnp.int32),
        pltpu.SemaphoreType.DMA,
    ]


def put_out(nz, nb, acc, out_refs):
    for s in range(nz):
        for b in range(nb):
            out_refs[s][:, b * BLK : (b + 1) * BLK] = acc[s * nb + b].astype(out_refs[s].dtype)


def form_kernel(nz, ny, nb, keep, fresh, place_ref, *refs):
    geos, refs = refs[:nz], refs[nz:]
    pays, refs = refs[:ny], refs[ny:]
    if fresh:
        fluxes, refs = refs[:ny], refs[ny:]
    outs, refs = refs[:nz], refs[nz:]
    if keep:
        tiles_ref, pairs, refs = refs[0], refs[1], refs[2:]
    row_feat, row_area, col_feat, col_area, flux, acc, slots_v, slots, sem, *more = refs
    if not keep:
        pairs = more[0]
    most = nz * ny * 2 * CAP
    width = slots.shape[1]
    for s in range(nz):
        g = geos[s][...].astype(F32)
        slots_v[s : s + 1, :] = g[14:15, :width].astype(jnp.int32)
    for m in range(ny):
        g = pays[m][0:GEO, :].astype(F32)
        slots_v[nz + m : nz + m + 1, :] = g[14:15, :width].astype(jnp.int32)
    copy = pltpu.make_async_copy(slots_v, slots, sem)
    copy.start()
    for s in range(nz):
        forms, h = row_features(geos[s][...].astype(F32))
        for b in range(nb):
            here = slice(b * BLK, (b + 1) * BLK)
            row_area[s * nb + b] = h[:, here]
            for v in range(3):
                row_feat[s * nb + b, v] = forms[v][:, here]
    acc[...] = jnp.zeros(acc.shape, F32)
    copy.wait()
    list_pairs(nz, ny, nb, place_ref, slots, pairs)
    depth = lax.broadcasted_iota(jnp.int32, (KDIM, LANES), 0)
    pick = jnp.where((depth >= 40) & (depth < 43), 1.0, 0.0).astype(BF16)
    for m in range(ny):
        feat = column_features(pays[m][0:GEO, :].astype(F32)).astype(BF16)
        for b in range(nb):
            here = slice(b * BLK, (b + 1) * BLK)
            turned = jnp.transpose(feat[:, here])
            col_feat[m * nb + b] = turned
            col_area[m * nb + b] = jnp.dot(turned, pick, preferred_element_type=F32)
            flux[m * nb + b] = fluxes[m][:, here] if fresh else pays[m][GEO:, here]
    count = pairs[most + SPARE]

    def tile_of(t):
        code = pairs[t]
        rb = jnp.minimum(code // 4096, nz * nb - 1)
        left = col_feat[code % 4096]
        f, s, q = (
            jnp.dot(left, row_feat[rb, v], preferred_element_type=F32) for v in range(3)
        )
        area = col_area[code % 4096]
        area = jnp.concatenate([area] * (BLK // LANES), axis=1) + row_area[rb]
        top = jnp.maximum(f, 0.0) * jnp.maximum(s, 0.0)
        return (top * pltpu.reciprocal(q * (math.pi * q - area), approx=True)).astype(BF16)

    if keep:

        def some(t, carry):
            for u in range(FORM_UNROLL):
                tiles_ref[t * FORM_UNROLL + u] = tile_of(t * FORM_UNROLL + u)
            return carry

        lax.fori_loop(0, (count + FORM_UNROLL - 1) // FORM_UNROLL, some, 0)
        apply_tiles(count, pairs, tiles_ref, flux, acc)
    else:

        def one(t, carry):
            code = pairs[t]
            acc[code // 4096] += jnp.dot(flux[code % 4096], tile_of(t), preferred_element_type=F32)
            return carry

        lax.fori_loop(0, count, one, 0)
    put_out(nz, nb, acc, outs)


def apply_tiles(count, pairs, tiles_ref, flux, acc):
    def some(t, carry):
        sums = []
        for u in range(APPLY_UNROLL):
            code = pairs[t * APPLY_UNROLL + u]
            tile = tiles_ref[t * APPLY_UNROLL + u]
            sums.append((code // 4096, jnp.dot(flux[code % 4096], tile, preferred_element_type=F32)))
        for rb, total in sums:
            acc[rb] += total
        return carry

    lax.fori_loop(0, (count + APPLY_UNROLL - 1) // APPLY_UNROLL, some, 0)


def apply_kernel(nz, ny, nb, pairs, tiles_ref, *refs):
    fluxes, refs = refs[:ny], refs[ny:]
    outs, refs = refs[:nz], refs[nz:]
    flux, acc = refs
    most = nz * ny * 2 * CAP
    for m in range(ny):
        for b in range(nb):
            flux[m * nb + b] = fluxes[m][:, b * BLK : (b + 1) * BLK]
    acc[...] = jnp.zeros(acc.shape, F32)
    apply_tiles(pairs[most + SPARE], pairs, tiles_ref, flux, acc)
    put_out(nz, nb, acc, outs)


def per_device(nz, ny, positions, normals, emission, material, area_level, reflect_table, area_table, pair_slots):
    patches = positions.shape[1]
    nb = patches // BLK
    most = nz * ny * 2 * CAP
    width = 2 * CAP * LANES
    keep = (most + SPARE) * BLK * BLK * 2 <= KEEP_BYTES
    params = [pltpu.CompilerParams(vmem_limit_bytes=n * 2**20) for n in ((30, 4) if keep else (60, 4))]
    place = jnp.stack([lax.axis_index("gx"), lax.axis_index("gy")]).astype(jnp.int32)
    slot_rows = jnp.transpose(pair_slots[0], (1, 2, 0))
    payload, geo, area = pl.pallas_call(
        pack_kernel,
        out_shape=(
            pltpu.VMEM((GEO + BANDS, patches), BF16),
            pltpu.VMEM((GEO, patches), BF16),
            jax.ShapeDtypeStruct((1, patches), F32),
        ),
        in_specs=[VMEM()] * 4 + [SMEM(), VMEM()],
        out_specs=(VMEM(),) * 3,
        scratch_shapes=[pltpu.VMEM((GEO, patches), F32)],
        name="pack",
    )(positions, normals, emission, area_level.reshape(1, patches), area_table, slot_rows)

    def along(x):
        return [lax.ppermute(x, "gx", [(i, (i + s) % nz) for i in range(nz)]) for s in range(1, nz)]

    def plane(x):
        got = {0: x}
        for m in range(2, ny, 2):
            got[m] = lax.ppermute(x, "gy", [(i, i ^ m) for i in range(ny)])
        for m in range(0, ny, 2):
            got[m + 1] = lax.ppermute(got[m], "gy", [(i, i ^ 1) for i in range(ny)])
        return [got[m] for m in range(ny)]

    def home(parts):
        total = parts[0]
        for s in range(1, nz):
            back = lax.ppermute(parts[s], "gx", [(i, (i - s) % nz) for i in range(nz)])
            total = total + back.astype(F32)
        return total

    rows = [geo] + along(geo)
    cols = plane(payload)
    out_parts = [jax.ShapeDtypeStruct((BANDS, patches), F32)] + [
        jax.ShapeDtypeStruct((BANDS, patches), BF16)
    ] * (nz - 1)

    def form(fluxes):
        fresh = fluxes is not None
        outs = list(out_parts)
        specs = [VMEM()] * nz
        if keep:
            outs += [
                pltpu.VMEM((most + SPARE, BLK, BLK), BF16),
                jax.ShapeDtypeStruct((most + SPARE + 1,), jnp.int32),
            ]
            specs += [VMEM(), SMEM()]
        scratch = form_scratch(nz, ny, nb, patches)
        if not keep:
            scratch += [pltpu.SMEM((most + SPARE + 1,), jnp.int32)]
        return pl.pallas_call(
            functools.partial(form_kernel, nz, ny, nb, keep, fresh),
            out_shape=tuple(outs),
            in_specs=[SMEM()] + [VMEM()] * (nz + ny + (ny if fresh else 0)),
            out_specs=tuple(specs),
            scratch_shapes=scratch,
            compiler_params=params[0],
            name="form",
        )(place, *rows, *cols, *(fluxes or []))

    def apply(pairs, tiles, fluxes):
        return pl.pallas_call(
            functools.partial(apply_kernel, nz, ny, nb),
            out_shape=tuple(out_parts),
            in_specs=[SMEM()] + [VMEM()] * (1 + ny),
            out_specs=(VMEM(),) * nz,
            scratch_shapes=[
                pltpu.VMEM((ny * nb, BANDS, BLK), BF16),
                pltpu.VMEM((nz * nb + 1, BANDS, BLK), F32),
            ],
            compiler_params=params[1],
            name="apply",
        )(pairs, tiles, *fluxes)

    kind_hot = (
        material[None, :] == jnp.arange(reflect_table.shape[0], dtype=jnp.int32)[:, None]
    ).astype(F32)
    reflect = jnp.dot(jnp.transpose(reflect_table), kind_hot, precision=lax.Precision.HIGHEST)

    first = form(None)
    radiosity = emission + reflect * home(first[:nz])
    fluxes = plane((area * radiosity).astype(BF16))
    second = apply(first[nz + 1], first[nz], fluxes) if keep else form(fluxes)
    return emission + reflect * home(second[:nz])


def solution(mesh):
    nz, ny = mesh.shape["gx"], mesh.shape["gy"]
    both = ("gx", "gy")
    placed = (
        P(None, both),
        P(None, both),
        P(None, both),
        P(both),
        P(both),
        P(),
        P(),
        P(both, None, None, None),
    )
    return jax.shard_map(
        functools.partial(per_device, nz, ny),
        mesh=mesh,
        in_specs=placed,
        out_specs=P(None, both),
        check_vma=False,
    )
```

```python
import functools
import math

import jax
import jax.numpy as jnp
from jax import lax
from jax.experimental import pallas as pl
from jax.experimental.pallas import tpu as pltpu
from jax.sharding import PartitionSpec as P

BANDS = 16
BLK = 256
CAP = 2
GEO = 16
LANES = 128
KDIM = 48
APPLY_UNROLL = 8
SPARE = 8
KEEP_BYTES = 24 * 2**20
BF16 = jnp.bfloat16
F32 = jnp.float32

VMEM = functools.partial(pl.BlockSpec, memory_space=pltpu.VMEM)
SMEM = functools.partial(pl.BlockSpec, memory_space=pltpu.SMEM)


def split(value, terms):
    out = []
    for _ in range(terms):
        part = value.astype(BF16).astype(F32)
        out.append(part)
        value = value - part
    return out


def pack_kernel(pos_ref, nrm_ref, emi_ref, level_ref, table_ref, slot_ref, pay_ref, geo_ref, area_ref, rows):
    level = level_ref[...]
    area = jnp.zeros(level.shape, F32)
    for k in range(table_ref.shape[0]):
        area = jnp.where(level == k, table_ref[k], area)
    area_ref[...] = area
    p1, p2 = split(pos_ref[...], 2)
    n1, n2 = split(nrm_ref[...], 2)
    a1, a2 = split(area, 2)
    rows[0:3, :] = p1
    rows[3:6, :] = p2
    rows[6:7, :] = a1
    rows[7:8, :] = a2
    rows[8:11, :] = n1
    rows[11:14, :] = n2
    rows[14:16, :] = jnp.zeros((2, area.shape[1]), F32)
    peers = slot_ref.shape[-1]
    for t in range(2 * CAP):
        rows[14:15, t * LANES : t * LANES + peers] = slot_ref[t // 2, t % 2 : t % 2 + 1, :].astype(F32)
    geo = rows[...].astype(BF16)
    geo_ref[...] = geo
    pay_ref[0:GEO, :] = geo
    pay_ref[GEO:, :] = (area * emi_ref[...]).astype(BF16)


def terms_of(g):
    pos, nrm = g[0:8], g[8:16]
    row = lax.broadcasted_iota(jnp.int32, pos.shape, 0)
    p = pos + pltpu.roll(pos, 5, 0)
    n = nrm + pltpu.roll(nrm, 5, 0)
    half = 0.5 * (pos[6:7] + pos[7:8])
    pp = jnp.sum(jnp.where(row < 3, p * p, 0.0), axis=0, keepdims=True)
    dot = jnp.sum(jnp.where(row < 3, n * p, 0.0), axis=0, keepdims=True)
    return pos, nrm, row, split(pp + half, 3), split(-dot, 3), (math.pi - 1.0) * half


def column_features(g):
    pos, nrm, row, q, c, h = terms_of(g)
    zero = jnp.zeros(pos.shape, F32)
    one = jnp.where(row == 6, 1.0, zero)
    pos = jnp.where(row < 6, pos, one)
    nrm = jnp.where(row < 6, nrm, one)
    consts, areas = zero, zero
    for t, value in enumerate(q + c):
        consts = jnp.where(row == t, value, consts)
    for t, value in enumerate(split(h, 3)):
        areas = jnp.where(row == t, value, areas)
    return jnp.concatenate([pos, nrm, pos, nrm, consts, areas], axis=0)


def row_features(g):
    pos, nrm, row, q, c, h = terms_of(g)
    zero = jnp.zeros(pos.shape, F32)

    def both(x):
        high = jnp.where(row < 3, x, pltpu.roll(x, 3, 0))
        low = jnp.where(row < 3, pltpu.roll(x, 5, 0), x)
        return jnp.where(row < 6, high, 0.0), jnp.where(row < 6, low, 0.0)

    def with_last(x, value):
        return jnp.where(row == 6, value, x)

    p_hi, p_lo = both(pos)
    n_hi, n_lo = both(nrm)
    facing = [with_last(n_hi, c[0]), with_last(zero, c[1]), with_last(n_lo, c[2]), zero, zero, zero]
    seen = [zero, p_hi, zero, p_lo, jnp.where((row >= 3) & (row < 6), 1.0, zero), zero]
    near = [
        with_last(-2.0 * p_hi, q[0]),
        with_last(zero, q[1]),
        with_last(-2.0 * p_lo, q[2]),
        zero,
        jnp.where(row < 3, 1.0, zero),
        zero,
    ]
    return [jnp.concatenate(parts, axis=0).astype(BF16) for parts in (facing, seen, near)], h


def sections(nz, ny):
    one = ny * 2 * CAP
    second = (nz - 1) * one + SPARE
    return second, second + one + SPARE


def list_pairs(nz, ny, nb, place_ref, slots, pairs):
    z, k = place_ref[0], place_ref[1]
    second, numbers = sections(nz, ny)

    def peer(s, m, count):
        zs = lax.rem(z - s + nz, nz)
        own = z * ny + jnp.bitwise_xor(k, m)
        served = zs * ny + k
        for t in range(CAP):
            row, col = slots[s, 2 * t * LANES + own], slots[s, (2 * t + 1) * LANES + own]
            pairs[count] = (s * nb + row) * 4096 + m * nb + col
            count = count + (row >= 0).astype(jnp.int32)
            col, row = slots[nz + m, 2 * t * LANES + served], slots[nz + m, (2 * t + 1) * LANES + served]
            pairs[count] = (s * nb + row) * 4096 + m * nb + col
            count = count + (row >= 0).astype(jnp.int32)
        return count

    for section, (start, lines) in enumerate(((0, range(1, nz)), (second, range(1)))):
        count = jnp.int32(start)
        for s in lines:
            if ny <= 8:
                for m in range(ny):
                    count = peer(s, m, count)
            else:
                count = lax.fori_loop(0, ny, functools.partial(peer, s), count)
        for t in range(SPARE):
            pairs[count + t] = nz * nb * 4096
        pairs[numbers + section] = count - start


def feature_scratch(nz, ny, nb):
    return [
        pltpu.VMEM((nz * nb, 3, KDIM, BLK), BF16),
        pltpu.VMEM((nz * nb, 1, BLK), F32),
        pltpu.VMEM((ny * nb, BLK, KDIM), BF16),
        pltpu.VMEM((ny * nb, BLK, LANES), F32),
        pltpu.VMEM((ny * nb, BANDS, BLK), BF16),
    ]


def own_scratch(nz, ny, nb):
    devices = -(-(nz + ny) // 8) * 8
    return [
        pltpu.VMEM((nz * nb + 1, BANDS, BLK), F32),
        pltpu.VMEM((devices, 2 * CAP * LANES), jnp.int32),
        pltpu.SMEM((devices, 2 * CAP * LANES), jnp.int32),
        pltpu.SemaphoreType.DMA,
    ]


def put_out(nb, acc, out_refs, first):
    for s, out in enumerate(out_refs):
        for b in range(nb):
            out[:, b * BLK : (b + 1) * BLK] = acc[(first + s) * nb + b].astype(out.dtype)


def prepare(nz, ny, nb, place_ref, geos, pays, fluxes, pairs, features, acc, slots_v, slots, sem):
    row_feat, row_area, col_feat, col_area, flux = features
    width = slots.shape[1]
    for s in range(nz):
        g = geos[s][...].astype(F32)
        slots_v[s : s + 1, :] = g[14:15, :width].astype(jnp.int32)
    for m in range(ny):
        g = pays[m][0:GEO, :].astype(F32)
        slots_v[nz + m : nz + m + 1, :] = g[14:15, :width].astype(jnp.int32)
    copy = pltpu.make_async_copy(slots_v, slots, sem)
    copy.start()
    for s in range(nz):
        forms, h = row_features(geos[s][...].astype(F32))
        for b in range(nb):
            here = slice(b * BLK, (b + 1) * BLK)
            row_area[s * nb + b] = h[:, here]
            for v in range(3):
                row_feat[s * nb + b, v] = forms[v][:, here]
    acc[...] = jnp.zeros(acc.shape, F32)
    copy.wait()
    list_pairs(nz, ny, nb, place_ref, slots, pairs)
    depth = lax.broadcasted_iota(jnp.int32, (KDIM, LANES), 0)
    pick = jnp.where((depth >= 40) & (depth < 43), 1.0, 0.0).astype(BF16)
    for m in range(ny):
        feat = column_features(pays[m][0:GEO, :].astype(F32)).astype(BF16)
        for b in range(nb):
            here = slice(b * BLK, (b + 1) * BLK)
            turned = jnp.transpose(feat[:, here])
            col_feat[m * nb + b] = turned
            col_area[m * nb + b] = jnp.dot(turned, pick, preferred_element_type=F32)
            flux[m * nb + b] = fluxes[m][:, here] if fluxes else pays[m][GEO:, here]


def tile_of(code, last, features):
    row_feat, row_area, col_feat, col_area, _ = features
    rb, cb = jnp.minimum(code // 4096, last), code % 4096
    left = col_feat[cb]
    f, s, q = (jnp.dot(left, row_feat[rb, v], preferred_element_type=F32) for v in range(3))
    area = col_area[cb]
    area = jnp.concatenate([area] * (BLK // LANES), axis=1) + row_area[rb]
    top = jnp.maximum(f, 0.0) * jnp.maximum(s, 0.0)
    return (top * pltpu.reciprocal(q * (math.pi * q - area), approx=True)).astype(BF16)


def form_tiles(unroll, first, count, last, pairs, features, tiles):
    def some(t, carry):
        for u in range(unroll):
            tiles[t * unroll + u] = tile_of(pairs[first + t * unroll + u], last, features)
        return carry

    lax.fori_loop(0, (count + unroll - 1) // unroll, some, 0)


def apply_tiles(first, count, spare, pairs, tiles, flux, acc):
    def some(t, carry):
        sums = []
        for u in range(APPLY_UNROLL):
            code = pairs[first + t * APPLY_UNROLL + u]
            tile = tiles[t * APPLY_UNROLL + u]
            sums.append((code // 4096, jnp.dot(flux[code % 4096], tile, preferred_element_type=F32)))
        for rb, total in sums:
            acc[jnp.minimum(rb, spare)] += total
        return carry

    lax.fori_loop(0, (count + APPLY_UNROLL - 1) // APPLY_UNROLL, some, 0)


def far_kernel(nz, ny, nb, place_ref, *refs):
    geos, pays, refs = refs[:nz], refs[nz : nz + ny], refs[nz + ny :]
    outs, refs = refs[: nz - 1], refs[nz - 1 :]
    tiles, pairs, features, own = refs[0], refs[1], refs[2:7], refs[7:]
    acc = own[0]
    _, numbers = sections(nz, ny)
    prepare(nz, ny, nb, place_ref, geos, pays, None, pairs, features, *own)
    count = pairs[numbers]
    form_tiles(8, 0, count, nz * nb - 1, pairs, features, tiles)
    apply_tiles(0, count, nz * nb, pairs, tiles, features[4], acc)
    put_out(nb, acc, outs, 1)


def near_kernel(nz, ny, nb, pairs, *refs):
    features, out, tiles, acc = refs[:5], refs[5], refs[6], refs[7]
    second, numbers = sections(nz, ny)
    count = pairs[numbers + 1]
    acc[...] = jnp.zeros(acc.shape, F32)
    form_tiles(4, second, count, nb - 1, pairs, features, tiles)
    apply_tiles(second, count, nb, pairs, tiles, features[4], acc)
    put_out(nb, acc, [out], 0)


def apply_kernel(nz, ny, nb, pairs, far_ref, near_ref, *refs):
    fluxes, refs = refs[:ny], refs[ny:]
    outs, refs = refs[:nz], refs[nz:]
    flux, acc = refs
    second, numbers = sections(nz, ny)
    for m in range(ny):
        for b in range(nb):
            flux[m * nb + b] = fluxes[m][:, b * BLK : (b + 1) * BLK]
    acc[...] = jnp.zeros(acc.shape, F32)
    apply_tiles(0, pairs[numbers], nz * nb, pairs, far_ref, flux, acc)
    apply_tiles(second, pairs[numbers + 1], nz * nb, pairs, near_ref, flux, acc)
    put_out(nb, acc, outs, 0)


def whole_kernel(nz, ny, nb, fresh, place_ref, *refs):
    geos, pays, refs = refs[:nz], refs[nz : nz + ny], refs[nz + ny :]
    fluxes, refs = (refs[:ny], refs[ny:]) if fresh else (None, refs)
    outs, features, own, pairs = refs[:nz], refs[nz : nz + 5], refs[nz + 5 : -1], refs[-1]
    acc, flux = own[0], features[4]
    second, numbers = sections(nz, ny)
    prepare(nz, ny, nb, place_ref, geos, pays, fluxes, pairs, features, *own)
    for section, start in enumerate((0, second)):

        def one(t, carry):
            code = pairs[start + t]
            tile = tile_of(code, nz * nb - 1, features)
            acc[code // 4096] += jnp.dot(flux[code % 4096], tile, preferred_element_type=F32)
            return carry

        lax.fori_loop(0, pairs[numbers + section], one, 0)
    put_out(nb, acc, outs, 0)


def per_device(nz, ny, positions, normals, emission, material, area_level, reflect_table, area_table, pair_slots):
    patches = positions.shape[1]
    nb = patches // BLK
    second, numbers = sections(nz, ny)
    keep = numbers * BLK * BLK * 2 <= KEEP_BYTES
    place = jnp.stack([lax.axis_index("gx"), lax.axis_index("gy")]).astype(jnp.int32)

    def call(kernel, name, megabytes, ins, outs, scratch, args):
        scalar = [getattr(x, "memory_space", None) == pltpu.SMEM for x in outs]
        spaces = [SMEM() if s else VMEM() for s in scalar]
        outs = [jax.ShapeDtypeStruct(x.shape, x.dtype) if s else x for x, s in zip(outs, scalar)]
        return pl.pallas_call(
            kernel,
            out_shape=tuple(outs),
            in_specs=ins,
            out_specs=tuple(spaces),
            scratch_shapes=scratch,
            compiler_params=megabytes and pltpu.CompilerParams(vmem_limit_bytes=megabytes * 2**20),
            name=name,
        )(*args)

    payload, geo, area = call(
        pack_kernel,
        "pack",
        None,
        [VMEM()] * 4 + [SMEM(), VMEM()],
        [
            pltpu.VMEM((GEO + BANDS, patches), BF16),
            pltpu.VMEM((GEO, patches), BF16),
            jax.ShapeDtypeStruct((1, patches), F32),
        ],
        [pltpu.VMEM((GEO, patches), F32)],
        (
            positions,
            normals,
            emission,
            area_level.reshape(1, patches),
            area_table,
            jnp.transpose(pair_slots[0], (1, 2, 0)),
        ),
    )

    def along(x):
        return [lax.ppermute(x, "gx", [(i, (i + s) % nz) for i in range(nz)]) for s in range(1, nz)]

    def plane(x):
        got = {0: x}
        for m in range(2, ny, 2):
            got[m] = lax.ppermute(x, "gy", [(i, i ^ m) for i in range(ny)])
        for m in range(0, ny, 2):
            got[m + 1] = lax.ppermute(got[m], "gy", [(i, i ^ 1) for i in range(ny)])
        return [got[m] for m in range(ny)]

    def sent(parts):
        return [
            lax.ppermute(part, "gx", [(i, (i - s) % nz) for i in range(nz)])
            for s, part in enumerate(parts, 1)
        ]

    def total(own, parts):
        for part in parts:
            own = own + part.astype(F32)
        return own

    own_part = jax.ShapeDtypeStruct((BANDS, patches), F32)
    far_parts = [jax.ShapeDtypeStruct((BANDS, patches), BF16)] * (nz - 1)
    features, own = feature_scratch(nz, ny, nb), own_scratch(nz, ny, nb)
    acc = own[0]
    pairs_list = pltpu.SMEM((numbers + 2,), jnp.int32)

    kind_hot = (
        material[None, :] == jnp.arange(reflect_table.shape[0], dtype=jnp.int32)[:, None]
    ).astype(F32)
    reflect = jnp.dot(jnp.transpose(reflect_table), kind_hot, precision=lax.Precision.HIGHEST)

    rows = [geo] + along(geo)
    cols = plane(payload)

    def whole(fluxes):
        got = call(
            functools.partial(whole_kernel, nz, ny, nb, bool(fluxes)),
            "whole",
            60,
            [SMEM()] + [VMEM()] * (nz + ny + len(fluxes)),
            [own_part] + far_parts,
            features + own + [pairs_list],
            (place, *rows, *cols, *fluxes),
        )
        return total(got[0], sent(got[1:]))

    if keep:
        got = call(
            functools.partial(far_kernel, nz, ny, nb),
            "far",
            16,
            [SMEM()] + [VMEM()] * (nz + ny),
            far_parts + [pltpu.VMEM((second, BLK, BLK), BF16), pairs_list] + features,
            own,
            (place, *rows, *cols),
        )
        returned = sent(got[: nz - 1])
        far_tiles, pairs, *kept = got[nz - 1 :]
        own_sum, near_tiles = call(
            functools.partial(near_kernel, nz, ny, nb),
            "near",
            8,
            [SMEM()] + [VMEM()] * 5,
            [own_part, pltpu.VMEM((numbers - second, BLK, BLK), BF16)],
            [pltpu.VMEM((nb + 1, BANDS, BLK), F32)],
            (pairs, *kept),
        )
        irradiation = total(own_sum, returned)
    else:
        irradiation = whole([])
    radiosity = emission + reflect * irradiation
    fluxes = plane((area * radiosity).astype(BF16))
    if keep:
        got = call(
            functools.partial(apply_kernel, nz, ny, nb),
            "apply",
            4,
            [SMEM()] + [VMEM()] * (2 + ny),
            [own_part] + far_parts,
            [features[4], acc],
            (pairs, far_tiles, near_tiles, *fluxes),
        )
        irradiation = total(got[0], sent(got[1:]))
    else:
        irradiation = whole(fluxes)
    return emission + reflect * irradiation


def solution(mesh):
    nz, ny = mesh.shape["gx"], mesh.shape["gy"]
    both = ("gx", "gy")
    placed = (
        P(None, both),
        P(None, both),
        P(None, both),
        P(both),
        P(both),
        P(),
        P(),
        P(both, None, None, None),
    )
    return jax.shard_map(
        functools.partial(per_device, nz, ny),
        mesh=mesh,
        in_specs=placed,
        out_specs=P(None, both),
        check_vma=False,
    )
```

```python
import functools
import math

import jax
import jax.numpy as jnp
from jax import lax
from jax.experimental import pallas as pl
from jax.experimental.pallas import tpu as pltpu
from jax.sharding import PartitionSpec as P

BANDS = 16
BLK = 256
CAP = 2
GEO = 16
LANES = 128
KDIM = 48
APPLY_UNROLL = 8
SPARE = 8
KEEP_BYTES = 24 * 2**20
BF16 = jnp.bfloat16
F32 = jnp.float32

VMEM = functools.partial(pl.BlockSpec, memory_space=pltpu.VMEM)
SMEM = functools.partial(pl.BlockSpec, memory_space=pltpu.SMEM)


def split(value, terms):
    out = []
    for _ in range(terms):
        part = value.astype(BF16).astype(F32)
        out.append(part)
        value = value - part
    return out


def pack_kernel(pos_ref, nrm_ref, emi_ref, level_ref, table_ref, slot_ref, pay_ref, geo_ref, area_ref, rows):
    level = level_ref[...]
    area = jnp.zeros(level.shape, F32)
    for k in range(table_ref.shape[1]):
        area = jnp.where(level == k, table_ref[:, k : k + 1], area)
    area_ref[...] = area
    p1, p2 = split(pos_ref[...], 2)
    n1, n2 = split(nrm_ref[...], 2)
    a1, a2 = split(area, 2)
    rows[0:3, :] = p1
    rows[3:6, :] = p2
    rows[6:7, :] = a1
    rows[7:8, :] = a2
    rows[8:11, :] = n1
    rows[11:14, :] = n2
    rows[14:16, :] = jnp.zeros((2, area.shape[1]), F32)
    peers = slot_ref.shape[-1]
    for t in range(2 * CAP):
        rows[14:15, t * LANES : t * LANES + peers] = slot_ref[t // 2, t % 2 : t % 2 + 1, :].astype(F32)
    geo = rows[...].astype(BF16)
    geo_ref[...] = geo
    pay_ref[0:GEO, :] = geo
    pay_ref[GEO:, :] = (area * emi_ref[...]).astype(BF16)


def terms_of(g):
    pos, nrm = g[0:8], g[8:16]
    row = lax.broadcasted_iota(jnp.int32, pos.shape, 0)
    p = pos + pltpu.roll(pos, 5, 0)
    n = nrm + pltpu.roll(nrm, 5, 0)
    half = 0.5 * (pos[6:7] + pos[7:8])
    pp = jnp.sum(jnp.where(row < 3, p * p, 0.0), axis=0, keepdims=True)
    dot = jnp.sum(jnp.where(row < 3, n * p, 0.0), axis=0, keepdims=True)
    return pos, nrm, row, split(pp + half, 3), split(-dot, 3), (math.pi - 1.0) * half


def column_features(g):
    pos, nrm, row, q, c, h = terms_of(g)
    zero = jnp.zeros(pos.shape, F32)
    one = jnp.where(row == 6, 1.0, zero)
    pos = jnp.where(row < 6, pos, one)
    nrm = jnp.where(row < 6, nrm, one)
    consts, areas = zero, zero
    for t, value in enumerate(q + c):
        consts = jnp.where(row == t, value, consts)
    for t, value in enumerate(split(h, 3)):
        areas = jnp.where(row == t, value, areas)
    return jnp.concatenate([pos, nrm, pos, nrm, consts, areas], axis=0)


def row_features(g):
    pos, nrm, row, q, c, h = terms_of(g)
    zero = jnp.zeros(pos.shape, F32)

    def both(x):
        high = jnp.where(row < 3, x, pltpu.roll(x, 3, 0))
        low = jnp.where(row < 3, pltpu.roll(x, 5, 0), x)
        return jnp.where(row < 6, high, 0.0), jnp.where(row < 6, low, 0.0)

    def with_last(x, value):
        return jnp.where(row == 6, value, x)

    p_hi, p_lo = both(pos)
    n_hi, n_lo = both(nrm)
    facing = [with_last(n_hi, c[0]), with_last(zero, c[1]), with_last(n_lo, c[2]), zero, zero, zero]
    seen = [zero, p_hi, zero, p_lo, jnp.where((row >= 3) & (row < 6), 1.0, zero), zero]
    near = [
        with_last(-2.0 * p_hi, q[0]),
        with_last(zero, q[1]),
        with_last(-2.0 * p_lo, q[2]),
        zero,
        jnp.where(row < 3, 1.0, zero),
        zero,
    ]
    return [jnp.concatenate(parts, axis=0).astype(BF16) for parts in (facing, seen, near)], h


def sections(nz, ny):
    one = ny * 2 * CAP
    second = (nz - 1) * one + 2 * SPARE
    return second, second + one + 2 * SPARE


def list_pairs(nz, ny, nb, slots, pairs):
    z, k = lax.axis_index("gx"), lax.axis_index("gy")
    second, bounds = sections(nz, ny)

    def peer(s, m, count):
        zs = lax.rem(z - s + nz, nz)
        own = z * ny + jnp.bitwise_xor(k, m)
        served = zs * ny + k
        for t in range(CAP):
            row, col = slots[s, 2 * t * LANES + own], slots[s, (2 * t + 1) * LANES + own]
            pairs[count] = (s * nb + row) * 4096 + m * nb + col
            count = count + (row >= 0).astype(jnp.int32)
            col, row = slots[nz + m, 2 * t * LANES + served], slots[nz + m, (2 * t + 1) * LANES + served]
            pairs[count] = (s * nb + row) * 4096 + m * nb + col
            count = count + (row >= 0).astype(jnp.int32)
        return count

    for start, lines in ((0, range(1, nz)), (second, range(1))):
        for t in range(SPARE):
            pairs[start + t] = nz * nb * 4096
        count = jnp.int32(start + SPARE)
        for s in lines:
            pairs[bounds + 2 * s] = count
            if ny <= 8:
                for m in range(ny):
                    count = peer(s, m, count)
            else:
                count = lax.fori_loop(0, ny, functools.partial(peer, s), count)
            pairs[bounds + 2 * s + 1] = count
        for t in range(SPARE):
            pairs[count + t] = nz * nb * 4096


def feature_scratch(nz, ny, nb):
    return [
        pltpu.VMEM((nz * nb, 3, KDIM, BLK), BF16),
        pltpu.VMEM((nz * nb, 1, BLK), F32),
        pltpu.VMEM((ny * nb, BLK, KDIM), BF16),
        pltpu.VMEM((ny * nb, BLK, LANES), F32),
        pltpu.VMEM((ny * nb, BANDS, BLK), BF16),
    ]


def own_scratch(nz, ny, nb):
    devices = -(-(nz + ny) // 8) * 8
    return [
        pltpu.VMEM((nz * nb + 1, BANDS, BLK), F32),
        pltpu.VMEM((devices, 2 * CAP * LANES), jnp.int32),
        pltpu.SMEM((devices, 2 * CAP * LANES), jnp.int32),
        pltpu.SemaphoreType.DMA,
    ]


def put_out(nb, acc, out_refs, first):
    for s, out in enumerate(out_refs):
        for b in range(nb):
            out[:, b * BLK : (b + 1) * BLK] = acc[(first + s) * nb + b].astype(out.dtype)


def prepare(nz, ny, nb, geos, pays, fluxes, pairs, features, acc, slots_v, slots, sem):
    row_feat, row_area, col_feat, col_area, flux = features
    width = slots.shape[1]
    for s in range(nz):
        g = geos[s][...].astype(F32)
        slots_v[s : s + 1, :] = g[14:15, :width].astype(jnp.int32)
    for m in range(ny):
        g = pays[m][0:GEO, :].astype(F32)
        slots_v[nz + m : nz + m + 1, :] = g[14:15, :width].astype(jnp.int32)
    copy = pltpu.make_async_copy(slots_v, slots, sem)
    copy.start()
    for s in range(nz):
        forms, h = row_features(geos[s][...].astype(F32))
        for b in range(nb):
            here = slice(b * BLK, (b + 1) * BLK)
            row_area[s * nb + b] = h[:, here]
            for v in range(3):
                row_feat[s * nb + b, v] = forms[v][:, here]
    acc[...] = jnp.zeros(acc.shape, F32)
    copy.wait()
    list_pairs(nz, ny, nb, slots, pairs)
    depth = lax.broadcasted_iota(jnp.int32, (KDIM, LANES), 0)
    pick = jnp.where((depth >= 40) & (depth < 43), 1.0, 0.0).astype(BF16)
    for m in range(ny):
        feat = column_features(pays[m][0:GEO, :].astype(F32)).astype(BF16)
        for b in range(nb):
            here = slice(b * BLK, (b + 1) * BLK)
            turned = jnp.transpose(feat[:, here])
            col_feat[m * nb + b] = turned
            col_area[m * nb + b] = jnp.dot(turned, pick, preferred_element_type=F32)
            flux[m * nb + b] = fluxes[m][:, here] if fluxes else pays[m][GEO:, here]


def tile_of(code, last, features):
    row_feat, row_area, col_feat, col_area, _ = features
    rb, cb = jnp.minimum(code // 4096, last), code % 4096
    left = col_feat[cb]
    f, s, q = (jnp.dot(left, row_feat[rb, v], preferred_element_type=F32) for v in range(3))
    area = col_area[cb]
    area = jnp.concatenate([area] * (BLK // LANES), axis=1) + row_area[rb]
    top = jnp.maximum(f, 0.0) * jnp.maximum(s, 0.0)
    return (top * pltpu.reciprocal(q * (math.pi * q - area), approx=True)).astype(BF16)


def form_and_apply(start, end, unroll, last, pairs, features, tiles, acc):
    flux = features[4]

    def add(step):
        sums = []
        for u in range(unroll):
            t = step * unroll + u
            code = pairs[start + t]
            total = jnp.dot(flux[code % 4096], tiles[t], preferred_element_type=F32)
            sums.append((jnp.minimum(code // 4096, last + 1), total))
        return sums

    def some(step, carry):
        sums = add(step - 1)
        for u in range(unroll):
            t = step * unroll + u
            tiles[t] = tile_of(pairs[start + t], last, features)
        for rb, total in sums:
            acc[rb] += total
        return carry

    first = SPARE // unroll
    steps = (end - start + unroll - 1) // unroll
    lax.fori_loop(first, steps, some, 0)
    for rb, total in add(steps - 1):
        acc[rb] += total


def apply_tiles(start, begin, end, spare, pairs, tiles, flux, acc):
    def some(step, carry):
        sums = []
        for u in range(APPLY_UNROLL):
            t = begin + step * APPLY_UNROLL + u
            code = pairs[t]
            total = jnp.dot(flux[code % 4096], tiles[t - start], preferred_element_type=F32)
            sums.append((jnp.where(t < end, (code // 4096) % spare, spare), total))
        for rb, total in sums:
            acc[rb] += total
        return carry

    lax.fori_loop(0, (end - begin + APPLY_UNROLL - 1) // APPLY_UNROLL, some, 0)


def far_kernel(nz, ny, nb, *refs):
    geos, pays, refs = refs[:nz], refs[nz : nz + ny], refs[nz + ny :]
    outs, refs = refs[: nz - 1], refs[nz - 1 :]
    tiles, pairs, features, own = refs[0], refs[1], refs[2:7], refs[7:]
    acc = own[0]
    _, bounds = sections(nz, ny)
    prepare(nz, ny, nb, geos, pays, None, pairs, features, *own)
    form_and_apply(0, pairs[bounds + 2 * nz - 1], 8, nz * nb - 1, pairs, features, tiles, acc)
    put_out(nb, acc, outs, 1)


def near_kernel(nz, ny, nb, pairs, *refs):
    features, out, tiles, acc = refs[:5], refs[5], refs[6], refs[7]
    second, bounds = sections(nz, ny)
    acc[...] = jnp.zeros(acc.shape, F32)
    form_and_apply(second, pairs[bounds + 1], 4, nb - 1, pairs, features, tiles, acc)
    put_out(nb, acc, [out], 0)


def apply_kernel(nz, ny, nb, s, pairs, tiles, *refs):
    fluxes, out, flux, acc = refs[:ny], *refs[ny:]
    second, bounds = sections(nz, ny)
    for m in range(ny):
        for b in range(nb):
            flux[m * nb + b] = fluxes[m][:, b * BLK : (b + 1) * BLK]
    acc[...] = jnp.zeros(acc.shape, F32)
    start = 0 if s else second
    apply_tiles(start, pairs[bounds + 2 * s], pairs[bounds + 2 * s + 1], nb, pairs, tiles, flux, acc)
    put_out(nb, acc, [out], 0)


def whole_kernel(nz, ny, nb, fresh, *refs):
    geos, pays, refs = refs[:nz], refs[nz : nz + ny], refs[nz + ny :]
    fluxes, refs = (refs[:ny], refs[ny:]) if fresh else (None, refs)
    outs, features, own, pairs = refs[:nz], refs[nz : nz + 5], refs[nz + 5 : -1], refs[-1]
    acc, flux = own[0], features[4]
    _, bounds = sections(nz, ny)
    prepare(nz, ny, nb, geos, pays, fluxes, pairs, features, *own)
    for s in range(nz):

        def one(t, carry):
            code = pairs[t]
            tile = tile_of(code, nz * nb - 1, features)
            acc[code // 4096] += jnp.dot(flux[code % 4096], tile, preferred_element_type=F32)
            return carry

        lax.fori_loop(pairs[bounds + 2 * s], pairs[bounds + 2 * s + 1], one, 0)
    put_out(nb, acc, outs, 0)


def per_device(nz, ny, positions, normals, emission, material, area_level, reflect_table, area_table, pair_slots):
    patches = positions.shape[1]
    nb = patches // BLK
    second, bounds = sections(nz, ny)
    keep = bounds * BLK * BLK * 2 <= KEEP_BYTES

    def call(kernel, name, megabytes, ins, outs, scratch, args):
        spaces = [SMEM() if getattr(x, "memory_space", None) == pltpu.SMEM else VMEM() for x in outs]
        return pl.pallas_call(
            kernel,
            out_shape=tuple(outs),
            in_specs=ins,
            out_specs=tuple(spaces),
            scratch_shapes=scratch,
            compiler_params=megabytes and pltpu.CompilerParams(vmem_limit_bytes=megabytes * 2**20),
            name=name,
        )(*args)

    payload, geo, area = call(
        pack_kernel,
        "pack",
        None,
        [VMEM()] * 6,
        [
            pltpu.VMEM((GEO + BANDS, patches), BF16),
            pltpu.VMEM((GEO, patches), BF16),
            jax.ShapeDtypeStruct((1, patches), F32),
        ],
        [pltpu.VMEM((GEO, patches), F32)],
        (
            positions,
            normals,
            emission,
            area_level.reshape(1, patches),
            area_table.reshape(1, -1),
            jnp.transpose(pair_slots[0], (1, 2, 0)),
        ),
    )

    def along(x):
        return [lax.ppermute(x, "gx", [(i, (i + s) % nz) for i in range(nz)]) for s in range(1, nz)]

    def plane(x, after=None):
        got = {0: x}
        for m in range(2, ny, 2):
            got[m] = lax.ppermute(x, "gy", [(i, i ^ m) for i in range(ny)])
        for m in range(0, ny, 2):
            held = got[m]
            if after is not None and m == 0:
                held, _ = lax.optimization_barrier((held, after))
            got[m + 1] = lax.ppermute(held, "gy", [(i, i ^ 1) for i in range(ny)])
        return [got[m] for m in range(ny)]

    def sent(parts):
        return [
            lax.ppermute(part, "gx", [(i, (i - s) % nz) for i in range(nz)])
            for s, part in enumerate(parts, 1)
        ]

    def total(own, parts):
        for part in parts:
            own = own + part.astype(F32)
        return own

    own_part = jax.ShapeDtypeStruct((BANDS, patches), F32)
    far_parts = [jax.ShapeDtypeStruct((BANDS, patches), BF16)] * (nz - 1)
    features, own = feature_scratch(nz, ny, nb), own_scratch(nz, ny, nb)
    acc = own[0]
    pairs_list = pltpu.SMEM((bounds + 2 * nz,), jnp.int32)

    kind_hot = (
        material[None, :] == jnp.arange(reflect_table.shape[0], dtype=jnp.int32)[:, None]
    ).astype(F32)
    reflect = jnp.dot(jnp.transpose(reflect_table), kind_hot, precision=lax.Precision.HIGHEST)

    rows = [geo] + along(geo)
    cols = plane(payload, rows[1])

    def whole(fluxes):
        got = call(
            functools.partial(whole_kernel, nz, ny, nb, bool(fluxes)),
            "whole",
            60,
            [VMEM()] * (nz + ny + len(fluxes)),
            [own_part] + far_parts,
            features + own + [pairs_list],
            (*rows, *cols, *fluxes),
        )
        return total(got[0], sent(got[1:]))

    if keep:
        got = call(
            functools.partial(far_kernel, nz, ny, nb),
            "far",
            16,
            [VMEM()] * (nz + ny),
            far_parts + [pltpu.VMEM((second, BLK, BLK), BF16), pairs_list] + features,
            own,
            (*rows, *cols),
        )
        returned = sent(got[: nz - 1])
        far_tiles, pairs, *kept = got[nz - 1 :]
        own_sum, near_tiles = call(
            functools.partial(near_kernel, nz, ny, nb),
            "near",
            8,
            [SMEM()] + [VMEM()] * 5,
            [own_part, pltpu.VMEM((bounds - second, BLK, BLK), BF16)],
            [pltpu.VMEM((nb + 1, BANDS, BLK), F32)],
            (pairs, *kept),
        )
        irradiation = total(own_sum, returned)
    else:
        irradiation = whole([])
    radiosity = emission + reflect * irradiation
    fluxes = plane((area * radiosity).astype(BF16))
    if keep:
        parts = [
            call(
                functools.partial(apply_kernel, nz, ny, nb, s),
                "apply",
                4,
                [SMEM()] + [VMEM()] * (1 + ny),
                [far_parts[0] if s else own_part],
                [features[4], pltpu.VMEM((nb + 1, BANDS, BLK), F32)],
                (pairs, far_tiles if s else near_tiles, *fluxes),
            )[0]
            for s in range(nz)
        ]
        irradiation = total(parts[0], sent(parts[1:]))
    else:
        irradiation = whole(fluxes)
    return emission + reflect * irradiation


def solution(mesh):
    nz, ny = mesh.shape["gx"], mesh.shape["gy"]
    both = ("gx", "gy")
    placed = (
        P(None, both),
        P(None, both),
        P(None, both),
        P(both),
        P(both),
        P(),
        P(),
        P(both, None, None, None),
    )
    return jax.shard_map(
        functools.partial(per_device, nz, ny),
        mesh=mesh,
        in_specs=placed,
        out_specs=P(None, both),
        check_vma=False,
    )
```

```python
import functools
import math

import jax
import jax.numpy as jnp
from jax import lax
from jax.experimental import pallas as pl
from jax.experimental.pallas import tpu as pltpu
from jax.sharding import PartitionSpec as P

BANDS = 16
BLK = 256
CAP = 2
GEO = 16
LANES = 128
KDIM = 48
APPLY_UNROLL = 8
SPARE = 8
FIRST_ORDER = {"m1": "z3", "m3": "z2", "m5": "z1"}
LATER_ORDER = {}
KEEP_BYTES = 24 * 2**20
BF16 = jnp.bfloat16
F32 = jnp.float32

VMEM = functools.partial(pl.BlockSpec, memory_space=pltpu.VMEM)
SMEM = functools.partial(pl.BlockSpec, memory_space=pltpu.SMEM)


def split(value, terms):
    out = []
    for _ in range(terms):
        part = value.astype(BF16).astype(F32)
        out.append(part)
        value = value - part
    return out


def pack_kernel(pos_ref, nrm_ref, emi_ref, level_ref, table_ref, slot_ref, pay_ref, geo_ref, area_ref, rows):
    level = level_ref[...]
    area = jnp.zeros(level.shape, F32)
    for k in range(table_ref.shape[1]):
        area = jnp.where(level == k, table_ref[:, k : k + 1], area)
    area_ref[...] = area
    p1, p2 = split(pos_ref[...], 2)
    n1, n2 = split(nrm_ref[...], 2)
    a1, a2 = split(area, 2)
    rows[0:3, :] = p1
    rows[3:6, :] = p2
    rows[6:7, :] = a1
    rows[7:8, :] = a2
    rows[8:11, :] = n1
    rows[11:14, :] = n2
    rows[14:16, :] = jnp.zeros((2, area.shape[1]), F32)
    peers = slot_ref.shape[-1]
    for t in range(2 * CAP):
        rows[14:15, t * LANES : t * LANES + peers] = slot_ref[t // 2, t % 2 : t % 2 + 1, :].astype(F32)
    geo = rows[...].astype(BF16)
    geo_ref[...] = geo
    pay_ref[0:GEO, :] = geo
    pay_ref[GEO:, :] = (area * emi_ref[...]).astype(BF16)


def terms_of(g):
    pos, nrm = g[0:8], g[8:16]
    row = lax.broadcasted_iota(jnp.int32, pos.shape, 0)
    p = pos + pltpu.roll(pos, 5, 0)
    n = nrm + pltpu.roll(nrm, 5, 0)
    half = 0.5 * (pos[6:7] + pos[7:8])
    pp = jnp.sum(jnp.where(row < 3, p * p, 0.0), axis=0, keepdims=True)
    dot = jnp.sum(jnp.where(row < 3, n * p, 0.0), axis=0, keepdims=True)
    area = (1.0 - 1.0 / math.pi) * half
    terms = split(jnp.where(row == 0, pp + half, jnp.where(row == 1, -dot, area)), 3)
    return pos, nrm, row, terms, area


def column_features(g):
    pos, nrm, row, terms, _ = terms_of(g)
    zero = jnp.zeros(pos.shape, F32)
    one = jnp.where(row == 6, 1.0, zero)
    pos = jnp.where(row < 6, pos, one)
    nrm = jnp.where(row < 6, nrm, one)
    later = jnp.where(row < 6, pltpu.roll(terms[1], 3, 0), pltpu.roll(terms[2], 6, 0))
    consts = jnp.where(row < 3, terms[0], later)
    return jnp.concatenate([pos, nrm, pos, nrm, consts, zero], axis=0)


def row_features(g):
    pos, nrm, row, terms, area = terms_of(g)
    zero = jnp.zeros(pos.shape, F32)

    def both(x):
        high = jnp.where(row < 3, x, pltpu.roll(x, 3, 0))
        low = jnp.where(row < 3, pltpu.roll(x, 5, 0), x)
        return jnp.where(row < 6, high, 0.0), jnp.where(row < 6, low, 0.0)

    def with_last(x, t, which):
        return jnp.where(row == 6, terms[t][which : which + 1], x)

    def ones(first):
        return jnp.where(row % 3 == first, 1.0, zero)

    p_hi, p_lo = both(pos)
    n_hi, n_lo = both(nrm)
    facing = [with_last(n_hi, 0, 1), with_last(zero, 1, 1), with_last(n_lo, 2, 1), zero, zero, zero]
    seen = [zero, p_hi, zero, p_lo, ones(1), zero]
    near = [
        with_last(-2.0 * p_hi, 0, 0),
        with_last(zero, 1, 0),
        with_last(-2.0 * p_lo, 2, 0),
        zero,
        ones(0),
        zero,
    ]
    return [jnp.concatenate(parts, axis=0).astype(BF16) for parts in (facing, seen, near)], area


def sections(nz, ny):
    one = ny * 2 * CAP
    second = (nz - 1) * one + 2 * SPARE
    return second, second + one + 2 * SPARE


def list_pairs(nz, ny, nb, slots, pairs):
    z, k = lax.axis_index("gx"), lax.axis_index("gy")
    second, bounds = sections(nz, ny)

    def peer(s, m, count):
        zs = lax.rem(z - s + nz, nz)
        own = z * ny + jnp.bitwise_xor(k, m)
        served = zs * ny + k
        for t in range(CAP):
            row, col = slots[s, 2 * t * LANES + own], slots[s, (2 * t + 1) * LANES + own]
            pairs[count] = (s * nb + row) * 4096 + m * nb + col
            count = count + (row >= 0).astype(jnp.int32)
            col, row = slots[nz + m, 2 * t * LANES + served], slots[nz + m, (2 * t + 1) * LANES + served]
            pairs[count] = (s * nb + row) * 4096 + m * nb + col
            count = count + (row >= 0).astype(jnp.int32)
        return count

    for start, lines in ((0, range(1, nz)), (second, range(1))):
        for t in range(SPARE):
            pairs[start + t] = nz * nb * 4096
        count = jnp.int32(start + SPARE)
        for s in lines:
            pairs[bounds + 2 * s] = count
            if ny <= 8:
                for m in range(ny):
                    count = peer(s, m, count)
            else:
                count = lax.fori_loop(0, ny, functools.partial(peer, s), count)
            pairs[bounds + 2 * s + 1] = count
        for t in range(SPARE):
            pairs[count + t] = nz * nb * 4096


def feature_scratch(nz, ny, nb):
    return [
        pltpu.VMEM((nz * nb, 3, KDIM, BLK), BF16),
        pltpu.VMEM((nz * nb, 1, BLK), F32),
        pltpu.VMEM((ny * nb, BLK, KDIM), BF16),
        pltpu.VMEM((ny * nb, BLK, LANES), F32),
        pltpu.VMEM((ny * nb, BANDS, BLK), BF16),
    ]


def own_scratch(nz, ny, nb):
    devices = -(-(nz + ny) // 8) * 8
    return [
        pltpu.VMEM((nz * nb + 1, BANDS, BLK), F32),
        pltpu.VMEM((devices, 2 * CAP * LANES), jnp.int32),
        pltpu.SMEM((devices, 2 * CAP * LANES), jnp.int32),
        pltpu.SemaphoreType.DMA,
    ]


def put_out(nb, acc, out_refs, first):
    for s, out in enumerate(out_refs):
        for b in range(nb):
            out[:, b * BLK : (b + 1) * BLK] = (acc[(first + s) * nb + b] * (1.0 / math.pi)).astype(out.dtype)


def prepare(nz, ny, nb, geos, pays, fluxes, pairs, features, acc, slots_v, slots, sem):
    row_feat, row_area, col_feat, col_area, flux = features
    width = slots.shape[1]
    for s in range(nz):
        g = geos[s][...].astype(F32)
        slots_v[s : s + 1, :] = g[14:15, :width].astype(jnp.int32)
    for m in range(ny):
        g = pays[m][0:GEO, :].astype(F32)
        slots_v[nz + m : nz + m + 1, :] = g[14:15, :width].astype(jnp.int32)
    copy = pltpu.make_async_copy(slots_v, slots, sem)
    copy.start()
    for s in range(nz):
        forms, h = row_features(geos[s][...].astype(F32))
        for b in range(nb):
            here = slice(b * BLK, (b + 1) * BLK)
            row_area[s * nb + b] = h[:, here]
            for v in range(3):
                row_feat[s * nb + b, v] = forms[v][:, here]
    acc[...] = jnp.zeros(acc.shape, F32)
    copy.wait()
    list_pairs(nz, ny, nb, slots, pairs)
    depth = lax.broadcasted_iota(jnp.int32, (KDIM, LANES), 0)
    pick = jnp.where((depth == 34) | (depth == 37), 1.0, 0.0).astype(BF16)
    for m in range(ny):
        feat = column_features(pays[m][0:GEO, :].astype(F32)).astype(BF16)
        for b in range(nb):
            here = slice(b * BLK, (b + 1) * BLK)
            turned = jnp.transpose(feat[:, here])
            col_feat[m * nb + b] = turned
            col_area[m * nb + b] = jnp.dot(turned, pick, preferred_element_type=F32)
            flux[m * nb + b] = fluxes[m][:, here] if fluxes else pays[m][GEO:, here]


def tile_of(code, last, features):
    row_feat, row_area, col_feat, col_area, _ = features
    rb, cb = jnp.minimum(code // 4096, last), code % 4096
    left = col_feat[cb]
    f, s, q = (jnp.dot(left, row_feat[rb, v], preferred_element_type=F32) for v in range(3))
    area = col_area[cb]
    area = jnp.concatenate([area] * (BLK // LANES), axis=1) + row_area[rb]
    top = jnp.maximum(f, 0.0) * jnp.maximum(s, 0.0)
    return (top * pltpu.reciprocal(q * (q - area), approx=True)).astype(BF16)


def form_and_apply(start, end, unroll, last, pairs, features, tiles, acc):
    flux = features[4]

    def add(step):
        sums = []
        for u in range(unroll):
            t = step * unroll + u
            code = pairs[start + t]
            total = jnp.dot(flux[code % 4096], tiles[t], preferred_element_type=F32)
            sums.append((jnp.minimum(code // 4096, last + 1), total))
        return sums

    def some(step, carry):
        sums = add(step - 1)
        for u in range(unroll):
            t = step * unroll + u
            tiles[t] = tile_of(pairs[start + t], last, features)
        for rb, total in sums:
            acc[rb] += total
        return carry

    first = SPARE // unroll
    steps = (end - start + unroll - 1) // unroll
    lax.fori_loop(first, steps, some, 0)
    for rb, total in add(steps - 1):
        acc[rb] += total


def apply_tiles(start, begin, end, spare, pairs, tiles, flux, acc):
    def some(step, carry):
        sums = []
        for u in range(APPLY_UNROLL):
            t = begin + step * APPLY_UNROLL + u
            code = pairs[t]
            total = jnp.dot(flux[code % 4096], tiles[t - start], preferred_element_type=F32)
            sums.append((jnp.where(t < end, (code // 4096) % spare, spare), total))
        for rb, total in sums:
            acc[rb] += total
        return carry

    lax.fori_loop(0, (end - begin + APPLY_UNROLL - 1) // APPLY_UNROLL, some, 0)


def far_kernel(nz, ny, nb, *refs):
    geos, pays, refs = refs[:nz], refs[nz : nz + ny], refs[nz + ny :]
    outs, refs = refs[: nz - 1], refs[nz - 1 :]
    tiles, pairs, features, own = refs[0], refs[1], refs[2:7], refs[7:]
    acc = own[0]
    _, bounds = sections(nz, ny)
    prepare(nz, ny, nb, geos, pays, None, pairs, features, *own)
    form_and_apply(0, pairs[bounds + 2 * nz - 1], 8, nz * nb - 1, pairs, features, tiles, acc)
    put_out(nb, acc, outs, 1)


def near_kernel(nz, ny, nb, pairs, *refs):
    features, out, tiles, acc = refs[:5], refs[5], refs[6], refs[7]
    second, bounds = sections(nz, ny)
    acc[...] = jnp.zeros(acc.shape, F32)
    form_and_apply(second, pairs[bounds + 1], 4, nb - 1, pairs, features, tiles, acc)
    put_out(nb, acc, [out], 0)


def apply_kernel(nz, ny, nb, s, pairs, tiles, *refs):
    fluxes, out, flux, acc = refs[:ny], *refs[ny:]
    second, bounds = sections(nz, ny)
    for m in range(ny):
        for b in range(nb):
            flux[m * nb + b] = fluxes[m][:, b * BLK : (b + 1) * BLK]
    acc[...] = jnp.zeros(acc.shape, F32)
    start = 0 if s else second
    apply_tiles(start, pairs[bounds + 2 * s], pairs[bounds + 2 * s + 1], nb, pairs, tiles, flux, acc)
    put_out(nb, acc, [out], 0)


def whole_kernel(nz, ny, nb, fresh, *refs):
    geos, pays, refs = refs[:nz], refs[nz : nz + ny], refs[nz + ny :]
    fluxes, refs = (refs[:ny], refs[ny:]) if fresh else (None, refs)
    outs, features, own, pairs = refs[:nz], refs[nz : nz + 5], refs[nz + 5 : -1], refs[-1]
    acc, flux = own[0], features[4]
    _, bounds = sections(nz, ny)
    prepare(nz, ny, nb, geos, pays, fluxes, pairs, features, *own)
    for s in range(nz):

        def one(t, carry):
            code = pairs[t]
            tile = tile_of(code, nz * nb - 1, features)
            acc[code // 4096] += jnp.dot(flux[code % 4096], tile, preferred_element_type=F32)
            return carry

        lax.fori_loop(pairs[bounds + 2 * s], pairs[bounds + 2 * s + 1], one, 0)
    put_out(nb, acc, outs, 0)


def per_device(nz, ny, positions, normals, emission, material, area_level, reflect_table, area_table, pair_slots):
    patches = positions.shape[1]
    nb = patches // BLK
    second, bounds = sections(nz, ny)
    keep = bounds * BLK * BLK * 2 <= KEEP_BYTES

    def call(kernel, name, megabytes, ins, outs, scratch, args):
        spaces = [SMEM() if getattr(x, "memory_space", None) == pltpu.SMEM else VMEM() for x in outs]
        return pl.pallas_call(
            kernel,
            out_shape=tuple(outs),
            in_specs=ins,
            out_specs=tuple(spaces),
            scratch_shapes=scratch,
            compiler_params=megabytes and pltpu.CompilerParams(vmem_limit_bytes=megabytes * 2**20),
            name=name,
        )(*args)

    payload, geo, area = call(
        pack_kernel,
        "pack",
        None,
        [VMEM()] * 6,
        [
            pltpu.VMEM((GEO + BANDS, patches), BF16),
            pltpu.VMEM((GEO, patches), BF16),
            jax.ShapeDtypeStruct((1, patches), F32),
        ],
        [pltpu.VMEM((GEO, patches), F32)],
        (
            positions,
            normals,
            emission,
            area_level.reshape(1, patches),
            area_table.reshape(1, -1),
            jnp.transpose(pair_slots[0], (1, 2, 0)),
        ),
    )

    def exchange(row_source, column_source, after):
        got = {"z0": row_source, "m0": column_source}
        todo = [] if row_source is None else [f"z{s}" for s in range(1, nz)]
        todo += [f"m{m}" for m in range(2, ny, 2)] + [f"m{m}" for m in range(1, ny, 2)]
        while todo:
            for name in list(todo):
                far, step = name[0] == "z", int(name[1:])
                source = "z0" if far else f"m{step - 1}" if step % 2 else "m0"
                if source not in got or after.get(name, source) not in got:
                    continue
                held = got[source]
                if name in after:
                    held, _ = lax.optimization_barrier((held, got[after[name]]))
                if far:
                    got[name] = lax.ppermute(held, "gx", [(i, (i + step) % nz) for i in range(nz)])
                else:
                    turn = 1 if step % 2 else step
                    got[name] = lax.ppermute(held, "gy", [(i, i ^ turn) for i in range(ny)])
                todo.remove(name)
        return got

    def sent(parts):
        return [
            lax.ppermute(part, "gx", [(i, (i - s) % nz) for i in range(nz)])
            for s, part in enumerate(parts, 1)
        ]

    def total(own, parts):
        for part in parts:
            own = own + part.astype(F32)
        return own

    own_part = jax.ShapeDtypeStruct((BANDS, patches), F32)
    far_parts = [jax.ShapeDtypeStruct((BANDS, patches), BF16)] * (nz - 1)
    features, own = feature_scratch(nz, ny, nb), own_scratch(nz, ny, nb)
    acc = own[0]
    pairs_list = pltpu.SMEM((bounds + 2 * nz,), jnp.int32)

    def exchange(row_source, column_source, after):
        got = {"z0": row_source, "m0": column_source}
        todo = [] if row_source is None else [f"z{s}" for s in range(1, nz)]
        todo += [f"m{m}" for m in range(2, ny, 2)] + [f"m{m}" for m in range(1, ny, 2)]
        while todo:
            for name in list(todo):
                far, step = name[0] == "z", int(name[1:])
                source = "z0" if far else f"m{step - 1}" if step % 2 else "m0"
                if source not in got or after.get(name, source) not in got:
                    continue
                held = got[source]
                if name in after:
                    held, _ = lax.optimization_barrier((held, got[after[name]]))
                if far:
                    got[name] = lax.ppermute(held, "gx", [(i, (i + step) % nz) for i in range(nz)])
                else:
                    turn = 1 if step % 2 else step
                    got[name] = lax.ppermute(held, "gy", [(i, i ^ turn) for i in range(ny)])
                todo.remove(name)
        return got

    def sent(parts):
        return [
            lax.ppermute(part, "gx", [(i, (i - s) % nz) for i in range(nz)])
            for s, part in enumerate(parts, 1)
        ]

    def total(own, parts):
        for part in parts:
            own = own + part.astype(F32)
        return own

    own_part = jax.ShapeDtypeStruct((BANDS, patches), F32)
    far_parts = [jax.ShapeDtypeStruct((BANDS, patches), BF16)] * (nz - 1)
    features, own = feature_scratch(nz, ny, nb), own_scratch(nz, ny, nb)
    acc = own[0]
    pairs_list = pltpu.SMEM((bounds + 2 * nz,), jnp.int32)

    kind_hot = (
        material[None, :] == jnp.arange(reflect_table.shape[0], dtype=jnp.int32)[:, None]
    ).astype(F32)
    reflect = jnp.dot(jnp.transpose(reflect_table), kind_hot, precision=lax.Precision.HIGHEST)

    ordered = nz == 4 and ny == 8
    got = exchange(geo, payload, FIRST_ORDER if ordered else {})
    rows, cols = [got[f"z{s}"] for s in range(nz)], [got[f"m{m}"] for m in range(ny)]


    def whole(fluxes):
        got = call(
            functools.partial(whole_kernel, nz, ny, nb, bool(fluxes)),
            "whole",
            60,
            [VMEM()] * (nz + ny + len(fluxes)),
            [own_part] + far_parts,
            features + own + [pairs_list],
            (*rows, *cols, *fluxes),
        )
        return total(got[0], sent(got[1:]))

    if keep:
        got = call(
            functools.partial(far_kernel, nz, ny, nb),
            "far",
            16,
            [VMEM()] * (nz + ny),
            far_parts + [pltpu.VMEM((second, BLK, BLK), BF16), pairs_list] + features,
            own,
            (*rows, *cols),
        )
        returned = sent(got[: nz - 1])
        far_tiles, pairs, *kept = got[nz - 1 :]
        own_sum, near_tiles = call(
            functools.partial(near_kernel, nz, ny, nb),
            "near",
            8,
            [SMEM()] + [VMEM()] * 5,
            [own_part, pltpu.VMEM((bounds - second, BLK, BLK), BF16)],
            [pltpu.VMEM((nb + 1, BANDS, BLK), F32)],
            (pairs, *kept),
        )
        irradiation = total(own_sum, returned)
    else:
        irradiation = whole([])
    radiosity = emission + reflect * irradiation
    got = exchange(None, (area * radiosity).astype(BF16), LATER_ORDER if ordered else {})
    fluxes = [got[f"m{m}"] for m in range(ny)]
    if keep:
        parts = [
            call(
                functools.partial(apply_kernel, nz, ny, nb, s),
                "apply",
                4,
                [SMEM()] + [VMEM()] * (1 + ny),
                [far_parts[0] if s else own_part],
                [features[4], pltpu.VMEM((nb + 1, BANDS, BLK), F32)],
                (pairs, far_tiles if s else near_tiles, *fluxes),
            )[0]
            for s in range(nz)
        ]
        irradiation = total(parts[0], sent(parts[1:]))
    else:
        irradiation = whole(fluxes)
    return emission + reflect * irradiation


def solution(mesh):
    nz, ny = mesh.shape["gx"], mesh.shape["gy"]
    both = ("gx", "gy")
    placed = (
        P(None, both),
        P(None, both),
        P(None, both),
        P(both),
        P(both),
        P(),
        P(),
        P(both, None, None, None),
    )
    return jax.shard_map(
        functools.partial(per_device, nz, ny),
        mesh=mesh,
        in_specs=placed,
        out_specs=P(None, both),
        check_vma=False,
    )
```

```python
import functools
import math

import jax
import jax.numpy as jnp
from jax import lax
from jax.experimental import pallas as pl
from jax.experimental.pallas import tpu as pltpu
from jax.sharding import PartitionSpec as P

BANDS = 16
BLK = 256
CAP = 2
GEO = 16
LANES = 128
KDIM = 48
APPLY_UNROLL = 8
SPARE = 8
FIRST_ORDER = {"m1": "z1", "m3": "z2", "m5": "z3"}
LATER_ORDER = {}
TOGETHER = [(1,), (2,), (3,), (0,)]
KEEP_BYTES = 24 * 2**20
BF16 = jnp.bfloat16
F32 = jnp.float32

VMEM = functools.partial(pl.BlockSpec, memory_space=pltpu.VMEM)
SMEM = functools.partial(pl.BlockSpec, memory_space=pltpu.SMEM)


def split(value, terms):
    out = []
    for _ in range(terms):
        part = value.astype(BF16).astype(F32)
        out.append(part)
        value = value - part
    return out


def pack_kernel(
    pos_ref, nrm_ref, emi_ref, level_ref, table_ref, kind_ref, share_ref, slot_ref, pay_ref, geo_ref, area_ref, reflect_ref, rows
):
    level = level_ref[...]
    area = jnp.zeros(level.shape, F32)
    for k in range(table_ref.shape[1]):
        area = jnp.where(level == k, table_ref[:, k : k + 1], area)
    area_ref[...] = area
    p1, p2 = split(pos_ref[...], 2)
    n1, n2 = split(nrm_ref[...], 2)
    a1, a2 = split(area, 2)
    rows[0:3, :] = p1
    rows[3:6, :] = p2
    rows[6:7, :] = a1
    rows[7:8, :] = a2
    rows[8:11, :] = n1
    rows[11:14, :] = n2
    rows[14:16, :] = jnp.zeros((2, area.shape[1]), F32)
    peers = slot_ref.shape[-1]
    for t in range(2 * CAP):
        rows[14:15, t * LANES : t * LANES + peers] = slot_ref[t // 2, t % 2 : t % 2 + 1, :].astype(F32)
    geo = rows[...].astype(BF16)
    geo_ref[...] = geo
    pay_ref[0:GEO, :] = geo
    pay_ref[GEO:, :] = (area * emi_ref[...]).astype(BF16)
    kind = jnp.broadcast_to(kind_ref[...], reflect_ref.shape)
    share = jnp.transpose(share_ref[...])
    reflect = jnp.zeros(reflect_ref.shape, F32)
    for k in range(share.shape[1]):
        reflect = jnp.where(kind == k, share[:, k : k + 1], reflect)
    reflect_ref[...] = reflect


def terms_of(g):
    pos, nrm = g[0:8], g[8:16]
    row = lax.broadcasted_iota(jnp.int32, pos.shape, 0)
    p = pos + pltpu.roll(pos, 5, 0)
    n = nrm + pltpu.roll(nrm, 5, 0)
    half = 0.5 * (pos[6:7] + pos[7:8])
    pp = jnp.sum(jnp.where(row < 3, p * p, 0.0), axis=0, keepdims=True)
    dot = jnp.sum(jnp.where(row < 3, n * p, 0.0), axis=0, keepdims=True)
    area = (1.0 - 1.0 / math.pi) * half
    terms = split(jnp.where(row == 0, pp + half, jnp.where(row == 1, -dot, area)), 3)
    return pos, nrm, row, terms, area


def column_features(g):
    pos, nrm, row, terms, _ = terms_of(g)
    zero = jnp.zeros(pos.shape, F32)
    one = jnp.where(row == 6, 1.0, zero)
    pos = jnp.where(row < 6, pos, one)
    nrm = jnp.where(row < 6, nrm, one)
    later = jnp.where(row < 6, pltpu.roll(terms[1], 3, 0), pltpu.roll(terms[2], 6, 0))
    consts = jnp.where(row < 3, terms[0], later)
    return jnp.concatenate([pos, nrm, pos, nrm, consts, zero], axis=0)


def row_features(g):
    pos, nrm, row, terms, area = terms_of(g)
    zero = jnp.zeros(pos.shape, F32)

    def both(x):
        high = jnp.where(row < 3, x, pltpu.roll(x, 3, 0))
        low = jnp.where(row < 3, pltpu.roll(x, 5, 0), x)
        return jnp.where(row < 6, high, 0.0), jnp.where(row < 6, low, 0.0)

    def with_last(x, t, which):
        return jnp.where(row == 6, terms[t][which : which + 1], x)

    def ones(first):
        return jnp.where(row % 3 == first, 1.0, zero)

    p_hi, p_lo = both(pos)
    n_hi, n_lo = both(nrm)
    facing = [with_last(n_hi, 0, 1), with_last(zero, 1, 1), with_last(n_lo, 2, 1), zero, zero, zero]
    seen = [zero, p_hi, zero, p_lo, ones(1), zero]
    near = [
        with_last(-2.0 * p_hi, 0, 0),
        with_last(zero, 1, 0),
        with_last(-2.0 * p_lo, 2, 0),
        zero,
        ones(0),
        zero,
    ]
    return [jnp.concatenate(parts, axis=0).astype(BF16) for parts in (facing, seen, near)], area


def sections(nz, ny):
    one = ny * 2 * CAP
    second = (nz - 1) * one + 2 * SPARE
    return second, second + one + 2 * SPARE


def list_pairs(nz, ny, nb, slots, pairs):
    z, k = lax.axis_index("gx"), lax.axis_index("gy")
    second, bounds = sections(nz, ny)

    def peer(s, m, count):
        zs = lax.rem(z - s + nz, nz)
        own = z * ny + jnp.bitwise_xor(k, m)
        served = zs * ny + k
        for t in range(CAP):
            row, col = slots[s, 2 * t * LANES + own], slots[s, (2 * t + 1) * LANES + own]
            pairs[count] = (s * nb + row) * 4096 + m * nb + col
            count = count + (row >= 0).astype(jnp.int32)
            col, row = slots[nz + m, 2 * t * LANES + served], slots[nz + m, (2 * t + 1) * LANES + served]
            pairs[count] = (s * nb + row) * 4096 + m * nb + col
            count = count + (row >= 0).astype(jnp.int32)
        return count

    for start, lines in ((0, range(1, nz)), (second, range(1))):
        for t in range(SPARE):
            pairs[start + t] = nz * nb * 4096
        count = jnp.int32(start + SPARE)
        for s in lines:
            pairs[bounds + 2 * s] = count
            if ny <= 8:
                for m in range(ny):
                    count = peer(s, m, count)
            else:
                count = lax.fori_loop(0, ny, functools.partial(peer, s), count)
            pairs[bounds + 2 * s + 1] = count
        for t in range(SPARE):
            pairs[count + t] = nz * nb * 4096


def feature_scratch(nz, ny, nb):
    return [
        pltpu.VMEM((nz * nb, 3, KDIM, BLK), BF16),
        pltpu.VMEM((nz * nb, 1, BLK), F32),
        pltpu.VMEM((ny * nb, BLK, KDIM), BF16),
        pltpu.VMEM((ny * nb, BLK, LANES), F32),
        pltpu.VMEM((ny * nb, BANDS, BLK), BF16),
    ]


def own_scratch(nz, ny, nb):
    devices = -(-(nz + ny) // 8) * 8
    return [
        pltpu.VMEM((nz * nb + 1, BANDS, BLK), F32),
        pltpu.VMEM((devices, 2 * CAP * LANES), jnp.int32),
        pltpu.SMEM((devices, 2 * CAP * LANES), jnp.int32),
        pltpu.SemaphoreType.DMA,
    ]


def put_out(nb, acc, out_refs, first):
    for s, out in enumerate(out_refs):
        for b in range(nb):
            out[:, b * BLK : (b + 1) * BLK] = (acc[(first + s) * nb + b] * (1.0 / math.pi)).astype(out.dtype)


def prepare(nz, ny, nb, geos, pays, fluxes, pairs, features, acc, slots_v, slots, sem):
    row_feat, row_area, col_feat, col_area, flux = features
    width = slots.shape[1]
    for s in range(nz):
        g = geos[s][...].astype(F32)
        slots_v[s : s + 1, :] = g[14:15, :width].astype(jnp.int32)
    for m in range(ny):
        g = pays[m][0:GEO, :].astype(F32)
        slots_v[nz + m : nz + m + 1, :] = g[14:15, :width].astype(jnp.int32)
    copy = pltpu.make_async_copy(slots_v, slots, sem)
    copy.start()
    for s in range(nz):
        forms, h = row_features(geos[s][...].astype(F32))
        for b in range(nb):
            here = slice(b * BLK, (b + 1) * BLK)
            row_area[s * nb + b] = h[:, here]
            for v in range(3):
                row_feat[s * nb + b, v] = forms[v][:, here]
    acc[...] = jnp.zeros(acc.shape, F32)
    copy.wait()
    list_pairs(nz, ny, nb, slots, pairs)
    depth = lax.broadcasted_iota(jnp.int32, (KDIM, LANES), 0)
    pick = jnp.where((depth == 34) | (depth == 37), 1.0, 0.0).astype(BF16)
    for m in range(ny):
        feat = column_features(pays[m][0:GEO, :].astype(F32)).astype(BF16)
        for b in range(nb):
            here = slice(b * BLK, (b + 1) * BLK)
            turned = jnp.transpose(feat[:, here])
            col_feat[m * nb + b] = turned
            col_area[m * nb + b] = jnp.dot(turned, pick, preferred_element_type=F32)
            flux[m * nb + b] = fluxes[m][:, here] if fluxes else pays[m][GEO:, here]


def tile_of(code, last, features):
    row_feat, row_area, col_feat, col_area, _ = features
    rb, cb = jnp.minimum(code // 4096, last), code % 4096
    left = col_feat[cb]
    f, s, q = (jnp.dot(left, row_feat[rb, v], preferred_element_type=F32) for v in range(3))
    area = col_area[cb]
    area = jnp.concatenate([area] * (BLK // LANES), axis=1) + row_area[rb]
    top = jnp.maximum(f, 0.0) * jnp.maximum(s, 0.0)
    return (top * pltpu.reciprocal(q * (q - area), approx=True)).astype(BF16)


def form_and_apply(start, end, unroll, last, pairs, features, tiles, acc):
    flux = features[4]

    def add(step):
        sums = []
        for u in range(unroll):
            t = step * unroll + u
            code = pairs[start + t]
            total = jnp.dot(flux[code % 4096], tiles[t], preferred_element_type=F32)
            sums.append((jnp.minimum(code // 4096, last + 1), total))
        return sums

    def some(step, carry):
        sums = add(step - 1)
        for u in range(unroll):
            t = step * unroll + u
            tiles[t] = tile_of(pairs[start + t], last, features)
        for rb, total in sums:
            acc[rb] += total
        return carry

    first = SPARE // unroll
    steps = (end - start + unroll - 1) // unroll
    lax.fori_loop(first, steps, some, 0)
    for rb, total in add(steps - 1):
        acc[rb] += total


def apply_tiles(start, begin, end, spare, pairs, tiles, flux, acc):
    def some(step, carry):
        sums = []
        for u in range(APPLY_UNROLL):
            t = begin + step * APPLY_UNROLL + u
            code = pairs[t]
            total = jnp.dot(flux[code % 4096], tiles[t - start], preferred_element_type=F32)
            sums.append((jnp.where(t < end, (code // 4096) % spare, spare), total))
        for rb, total in sums:
            acc[rb] += total
        return carry

    lax.fori_loop(0, (end - begin + APPLY_UNROLL - 1) // APPLY_UNROLL, some, 0)


def far_kernel(nz, ny, nb, *refs):
    geos, pays, refs = refs[:nz], refs[nz : nz + ny], refs[nz + ny :]
    outs, refs = refs[: nz - 1], refs[nz - 1 :]
    tiles, pairs, features, own = refs[0], refs[1], refs[2:7], refs[7:]
    acc = own[0]
    _, bounds = sections(nz, ny)
    prepare(nz, ny, nb, geos, pays, None, pairs, features, *own)
    form_and_apply(0, pairs[bounds + 2 * nz - 1], 8, nz * nb - 1, pairs, features, tiles, acc)
    put_out(nb, acc, outs, 1)


def near_kernel(nz, ny, nb, pairs, *refs):
    features, out, tiles, acc = refs[:5], refs[5], refs[6], refs[7]
    second, bounds = sections(nz, ny)
    acc[...] = jnp.zeros(acc.shape, F32)
    form_and_apply(second, pairs[bounds + 1], 4, nb - 1, pairs, features, tiles, acc)
    put_out(nb, acc, [out], 0)


def apply_kernel(nz, ny, nb, lines, pairs, *refs):
    tiles, refs = refs[: len(lines)], refs[len(lines) :]
    fluxes, outs, flux, acc = refs[:ny], refs[ny:-2], *refs[-2:]
    second, bounds = sections(nz, ny)
    for m in range(ny):
        for b in range(nb):
            flux[m * nb + b] = fluxes[m][:, b * BLK : (b + 1) * BLK]
    for s, tile, out in zip(lines, tiles, outs):
        acc[...] = jnp.zeros(acc.shape, F32)
        start = 0 if s else second
        apply_tiles(start, pairs[bounds + 2 * s], pairs[bounds + 2 * s + 1], nb, pairs, tile, flux, acc)
        put_out(nb, acc, [out], 0)


def whole_kernel(nz, ny, nb, fresh, *refs):
    geos, pays, refs = refs[:nz], refs[nz : nz + ny], refs[nz + ny :]
    fluxes, refs = (refs[:ny], refs[ny:]) if fresh else (None, refs)
    outs, features, own, pairs = refs[:nz], refs[nz : nz + 5], refs[nz + 5 : -1], refs[-1]
    acc, flux = own[0], features[4]
    _, bounds = sections(nz, ny)
    prepare(nz, ny, nb, geos, pays, fluxes, pairs, features, *own)
    for s in range(nz):

        def one(t, carry):
            code = pairs[t]
            tile = tile_of(code, nz * nb - 1, features)
            acc[code // 4096] += jnp.dot(flux[code % 4096], tile, preferred_element_type=F32)
            return carry

        lax.fori_loop(pairs[bounds + 2 * s], pairs[bounds + 2 * s + 1], one, 0)
    put_out(nb, acc, outs, 0)


def per_device(nz, ny, positions, normals, emission, material, area_level, reflect_table, area_table, pair_slots):
    patches = positions.shape[1]
    nb = patches // BLK
    second, bounds = sections(nz, ny)
    keep = bounds * BLK * BLK * 2 <= KEEP_BYTES

    def call(kernel, name, megabytes, ins, outs, scratch, args):
        spaces = [SMEM() if getattr(x, "memory_space", None) == pltpu.SMEM else VMEM() for x in outs]
        return pl.pallas_call(
            kernel,
            out_shape=tuple(outs),
            in_specs=ins,
            out_specs=tuple(spaces),
            scratch_shapes=scratch,
            compiler_params=megabytes and pltpu.CompilerParams(vmem_limit_bytes=megabytes * 2**20),
            name=name,
        )(*args)

    payload, geo, area, reflect = call(
        pack_kernel,
        "pack",
        None,
        [VMEM()] * 8,
        [
            pltpu.VMEM((GEO + BANDS, patches), BF16),
            pltpu.VMEM((GEO, patches), BF16),
            pltpu.VMEM((1, patches), F32),
            pltpu.VMEM((BANDS, patches), F32),
        ],
        [pltpu.VMEM((GEO, patches), F32)],
        (
            positions,
            normals,
            emission,
            area_level.reshape(1, patches),
            area_table.reshape(1, -1),
            material.reshape(1, patches),
            reflect_table,
            jnp.transpose(pair_slots[0], (1, 2, 0)),
        ),
    )

    def exchange(row_source, column_source, after):
        got = {"z0": row_source, "m0": column_source}
        todo = [] if row_source is None else [f"z{s}" for s in range(1, nz)]
        todo += [f"m{m}" for m in range(2, ny, 2)] + [f"m{m}" for m in range(1, ny, 2)]
        while todo:
            for name in list(todo):
                far, step = name[0] == "z", int(name[1:])
                source = "z0" if far else f"m{step - 1}" if step % 2 else "m0"
                if source not in got or after.get(name, source) not in got:
                    continue
                held = got[source]
                if name in after:
                    held, _ = lax.optimization_barrier((held, got[after[name]]))
                if far:
                    got[name] = lax.ppermute(held, "gx", [(i, (i + step) % nz) for i in range(nz)])
                else:
                    turn = 1 if step % 2 else step
                    got[name] = lax.ppermute(held, "gy", [(i, i ^ turn) for i in range(ny)])
                todo.remove(name)
        return got

    def sent(parts):
        return [
            lax.ppermute(part, "gx", [(i, (i - s) % nz) for i in range(nz)])
            for s, part in enumerate(parts, 1)
        ]

    def total(own, parts):
        for part in parts:
            own = own + part.astype(F32)
        return own

    own_part = jax.ShapeDtypeStruct((BANDS, patches), F32)
    far_parts = [jax.ShapeDtypeStruct((BANDS, patches), BF16)] * (nz - 1)
    features, own = feature_scratch(nz, ny, nb), own_scratch(nz, ny, nb)
    acc = own[0]
    pairs_list = pltpu.SMEM((bounds + 2 * nz,), jnp.int32)

    ordered = nz == 4 and ny == 8
    got = exchange(geo, payload, FIRST_ORDER if ordered else {})
    rows, cols = [got[f"z{s}"] for s in range(nz)], [got[f"m{m}"] for m in range(ny)]

    def whole(fluxes):
        got = call(
            functools.partial(whole_kernel, nz, ny, nb, bool(fluxes)),
            "whole",
            60,
            [VMEM()] * (nz + ny + len(fluxes)),
            [own_part] + far_parts,
            features + own + [pairs_list],
            (*rows, *cols, *fluxes),
        )
        return total(got[0], sent(got[1:]))

    if keep:
        got = call(
            functools.partial(far_kernel, nz, ny, nb),
            "far",
            16,
            [VMEM()] * (nz + ny),
            far_parts + [pltpu.VMEM((second, BLK, BLK), BF16), pairs_list] + features,
            own,
            (*rows, *cols),
        )
        returned = sent(got[: nz - 1])
        far_tiles, pairs, *kept = got[nz - 1 :]
        own_sum, near_tiles = call(
            functools.partial(near_kernel, nz, ny, nb),
            "near",
            8,
            [SMEM()] + [VMEM()] * 5,
            [own_part, pltpu.VMEM((bounds - second, BLK, BLK), BF16)],
            [pltpu.VMEM((nb + 1, BANDS, BLK), F32)],
            (pairs, *kept),
        )
        irradiation = total(own_sum, returned)
    else:
        irradiation = whole([])
    radiosity = emission + reflect * irradiation
    got = exchange(None, (area * radiosity).astype(BF16), LATER_ORDER if ordered else {})
    fluxes = [got[f"m{m}"] for m in range(ny)]
    if keep:
        parts = {}
        for lines in TOGETHER if ordered else [range(1, nz), [0]]:
            got = call(
                functools.partial(apply_kernel, nz, ny, nb, lines),
                "apply",
                4,
                [SMEM()] + [VMEM()] * (len(lines) + ny),
                [far_parts[0] if s else own_part for s in lines],
                [features[4], pltpu.VMEM((nb + 1, BANDS, BLK), F32)],
                (pairs, *[far_tiles if s else near_tiles for s in lines], *fluxes),
            )
            parts.update(zip(lines, got))
        irradiation = total(parts[0], sent([parts[s] for s in range(1, nz)]))
    else:
        irradiation = whole(fluxes)
    return emission + reflect * irradiation


def solution(mesh):
    nz, ny = mesh.shape["gx"], mesh.shape["gy"]
    both = ("gx", "gy")
    placed = (
        P(None, both),
        P(None, both),
        P(None, both),
        P(both),
        P(both),
        P(),
        P(),
        P(both, None, None, None),
    )
    return jax.shard_map(
        functools.partial(per_device, nz, ny),
        mesh=mesh,
        in_specs=placed,
        out_specs=P(None, both),
        check_vma=False,
    )
```

```python
import functools
import math

import jax
import jax.numpy as jnp
from jax import lax
from jax.experimental import pallas as pl
from jax.experimental.pallas import tpu as pltpu
from jax.sharding import PartitionSpec as P

BANDS = 16
BLK = 256
CAP = 2
GEO = 16
LANES = 128
KDIM = 48
APPLY_UNROLL = 8
SPARE = 8
FIRST_ORDER = {"m1": "z1", "m3": "z2", "m5": "z3"}
LATER_ORDER = {}
TOGETHER = [(1,), (2,), (3,), (0,)]
KEEP_BYTES = 24 * 2**20
BF16 = jnp.bfloat16
F32 = jnp.float32

VMEM = functools.partial(pl.BlockSpec, memory_space=pltpu.VMEM)
SMEM = functools.partial(pl.BlockSpec, memory_space=pltpu.SMEM)


def split(value, terms):
    out = []
    for _ in range(terms):
        part = value.astype(BF16).astype(F32)
        out.append(part)
        value = value - part
    return out


def pack_kernel(
    pos_ref, nrm_ref, emi_ref, level_ref, table_ref, kind_ref, share_ref, slot_ref, pay_ref, geo_ref, area_ref, reflect_ref, kept_ref, rows
):
    level = level_ref[...]
    area = jnp.zeros(level.shape, F32)
    for k in range(table_ref.shape[1]):
        area = jnp.where(level == k, table_ref[:, k : k + 1], area)
    area_ref[...] = area
    p1, p2 = split(pos_ref[...], 2)
    n1, n2 = split(nrm_ref[...], 2)
    a1, a2 = split(area, 2)
    rows[0:3, :] = p1
    rows[3:6, :] = p2
    rows[6:7, :] = a1
    rows[7:8, :] = a2
    rows[8:11, :] = n1
    rows[11:14, :] = n2
    rows[14:16, :] = jnp.zeros((2, area.shape[1]), F32)
    peers = slot_ref.shape[-1]
    for t in range(2 * CAP):
        rows[14:15, t * LANES : t * LANES + peers] = slot_ref[t // 2, t % 2 : t % 2 + 1, :].astype(F32)
    geo = rows[...].astype(BF16)
    geo_ref[...] = geo
    pay_ref[0:GEO, :] = geo
    pay_ref[GEO:, :] = (area * emi_ref[...]).astype(BF16)
    kind = jnp.broadcast_to(kind_ref[...], reflect_ref.shape)
    share = jnp.transpose(share_ref[...])
    reflect = jnp.zeros(reflect_ref.shape, F32)
    for k in range(share.shape[1]):
        reflect = jnp.where(kind == k, share[:, k : k + 1], reflect)
    reflect_ref[...] = reflect
    kept_ref[...] = emi_ref[...]


def terms_of(g):
    pos, nrm = g[0:8], g[8:16]
    row = lax.broadcasted_iota(jnp.int32, pos.shape, 0)
    p = pos + pltpu.roll(pos, 5, 0)
    n = nrm + pltpu.roll(nrm, 5, 0)
    half = 0.5 * (pos[6:7] + pos[7:8])
    pp = jnp.sum(jnp.where(row < 3, p * p, 0.0), axis=0, keepdims=True)
    dot = jnp.sum(jnp.where(row < 3, n * p, 0.0), axis=0, keepdims=True)
    area = (1.0 - 1.0 / math.pi) * half
    terms = split(jnp.where(row == 0, pp + half, jnp.where(row == 1, -dot, area)), 3)
    return pos, nrm, row, terms, area


def column_features(g):
    pos, nrm, row, terms, _ = terms_of(g)
    zero = jnp.zeros(pos.shape, F32)
    one = jnp.where(row == 6, 1.0, zero)
    pos = jnp.where(row < 6, pos, one)
    nrm = jnp.where(row < 6, nrm, one)
    later = jnp.where(row < 6, pltpu.roll(terms[1], 3, 0), pltpu.roll(terms[2], 6, 0))
    consts = jnp.where(row < 3, terms[0], later)
    return jnp.concatenate([pos, nrm, pos, nrm, consts, zero], axis=0)


def row_features(g):
    pos, nrm, row, terms, area = terms_of(g)
    zero = jnp.zeros(pos.shape, F32)

    def both(x):
        high = jnp.where(row < 3, x, pltpu.roll(x, 3, 0))
        low = jnp.where(row < 3, pltpu.roll(x, 5, 0), x)
        return jnp.where(row < 6, high, 0.0), jnp.where(row < 6, low, 0.0)

    def with_last(x, t, which):
        return jnp.where(row == 6, terms[t][which : which + 1], x)

    def ones(first):
        return jnp.where(row % 3 == first, 1.0, zero)

    p_hi, p_lo = both(pos)
    n_hi, n_lo = both(nrm)
    facing = [with_last(n_hi, 0, 1), with_last(zero, 1, 1), with_last(n_lo, 2, 1), zero, zero, zero]
    seen = [zero, p_hi, zero, p_lo, ones(1), zero]
    near = [
        with_last(-2.0 * p_hi, 0, 0),
        with_last(zero, 1, 0),
        with_last(-2.0 * p_lo, 2, 0),
        zero,
        ones(0),
        zero,
    ]
    return [jnp.concatenate(parts, axis=0).astype(BF16) for parts in (facing, seen, near)], area


def sections(nz, ny):
    one = ny * 2 * CAP
    second = (nz - 1) * one + 2 * SPARE
    return second, second + one + 2 * SPARE


def list_pairs(nz, ny, nb, slots, pairs):
    z, k = lax.axis_index("gx"), lax.axis_index("gy")
    second, bounds = sections(nz, ny)

    def peer(s, m, count):
        zs = lax.rem(z - s + nz, nz)
        own = z * ny + jnp.bitwise_xor(k, m)
        served = zs * ny + k
        for t in range(CAP):
            row, col = slots[s, 2 * t * LANES + own], slots[s, (2 * t + 1) * LANES + own]
            pairs[count] = (s * nb + row) * 4096 + m * nb + col
            count = count + (row >= 0).astype(jnp.int32)
            col, row = slots[nz + m, 2 * t * LANES + served], slots[nz + m, (2 * t + 1) * LANES + served]
            pairs[count] = (s * nb + row) * 4096 + m * nb + col
            count = count + (row >= 0).astype(jnp.int32)
        return count

    for start, lines in ((0, range(1, nz)), (second, range(1))):
        for t in range(SPARE):
            pairs[start + t] = nz * nb * 4096
        count = jnp.int32(start + SPARE)
        for s in lines:
            pairs[bounds + 2 * s] = count
            if ny <= 8:
                for m in range(ny):
                    count = peer(s, m, count)
            else:
                count = lax.fori_loop(0, ny, functools.partial(peer, s), count)
            pairs[bounds + 2 * s + 1] = count
        for t in range(SPARE):
            pairs[count + t] = nz * nb * 4096


def feature_scratch(nz, ny, nb):
    return [
        pltpu.VMEM((nz * nb, 3, KDIM, BLK), BF16),
        pltpu.VMEM((nz * nb, 1, BLK), F32),
        pltpu.VMEM((ny * nb, BLK, KDIM), BF16),
        pltpu.VMEM((ny * nb, BLK, LANES), F32),
        pltpu.VMEM((ny * nb, BANDS, BLK), BF16),
    ]


def own_scratch(nz, ny, nb):
    devices = -(-(nz + ny) // 8) * 8
    return [
        pltpu.VMEM((nz * nb + 1, BANDS, BLK), F32),
        pltpu.VMEM((devices, 2 * CAP * LANES), jnp.int32),
        pltpu.SMEM((devices, 2 * CAP * LANES), jnp.int32),
        pltpu.SemaphoreType.DMA,
    ]


def put_out(nb, acc, out_refs, first):
    for s, out in enumerate(out_refs):
        for b in range(nb):
            out[:, b * BLK : (b + 1) * BLK] = (acc[(first + s) * nb + b] * (1.0 / math.pi)).astype(out.dtype)


def prepare(nz, ny, nb, geos, pays, fluxes, pairs, features, acc, slots_v, slots, sem):
    row_feat, row_area, col_feat, col_area, flux = features
    width = slots.shape[1]
    for s in range(nz):
        g = geos[s][...].astype(F32)
        slots_v[s : s + 1, :] = g[14:15, :width].astype(jnp.int32)
    for m in range(ny):
        g = pays[m][0:GEO, :].astype(F32)
        slots_v[nz + m : nz + m + 1, :] = g[14:15, :width].astype(jnp.int32)
    copy = pltpu.make_async_copy(slots_v, slots, sem)
    copy.start()
    for s in range(nz):
        forms, h = row_features(geos[s][...].astype(F32))
        for b in range(nb):
            here = slice(b * BLK, (b + 1) * BLK)
            row_area[s * nb + b] = h[:, here]
            for v in range(3):
                row_feat[s * nb + b, v] = forms[v][:, here]
    acc[...] = jnp.zeros(acc.shape, F32)
    copy.wait()
    list_pairs(nz, ny, nb, slots, pairs)
    depth = lax.broadcasted_iota(jnp.int32, (KDIM, LANES), 0)
    pick = jnp.where((depth == 34) | (depth == 37), 1.0, 0.0).astype(BF16)
    for m in range(ny):
        feat = column_features(pays[m][0:GEO, :].astype(F32)).astype(BF16)
        for b in range(nb):
            here = slice(b * BLK, (b + 1) * BLK)
            turned = jnp.transpose(feat[:, here])
            col_feat[m * nb + b] = turned
            col_area[m * nb + b] = jnp.dot(turned, pick, preferred_element_type=F32)
            flux[m * nb + b] = fluxes[m][:, here] if fluxes else pays[m][GEO:, here]


def tile_of(code, last, features):
    row_feat, row_area, col_feat, col_area, _ = features
    rb, cb = jnp.minimum(code // 4096, last), code % 4096
    left = col_feat[cb]
    f, s, q = (jnp.dot(left, row_feat[rb, v], preferred_element_type=F32) for v in range(3))
    area = col_area[cb]
    area = jnp.concatenate([area] * (BLK // LANES), axis=1) + row_area[rb]
    top = jnp.maximum(f, 0.0) * jnp.maximum(s, 0.0)
    return (top * pltpu.reciprocal(q * (q - area), approx=True)).astype(BF16)


def form_and_apply(start, end, unroll, last, pairs, features, tiles, acc):
    flux = features[4]

    def add(step):
        sums = []
        for u in range(unroll):
            t = step * unroll + u
            code = pairs[start + t]
            total = jnp.dot(flux[code % 4096], tiles[t], preferred_element_type=F32)
            sums.append((jnp.minimum(code // 4096, last + 1), total))
        return sums

    def some(step, carry):
        sums = add(step - 1)
        for u in range(unroll):
            t = step * unroll + u
            tiles[t] = tile_of(pairs[start + t], last, features)
        for rb, total in sums:
            acc[rb] += total
        return carry

    first = SPARE // unroll
    steps = (end - start + unroll - 1) // unroll
    lax.fori_loop(first, steps, some, 0)
    for rb, total in add(steps - 1):
        acc[rb] += total


def apply_tiles(start, begin, end, spare, pairs, tiles, flux, acc):
    def some(step, carry):
        sums = []
        for u in range(APPLY_UNROLL):
            t = begin + step * APPLY_UNROLL + u
            code = pairs[t]
            total = jnp.dot(flux[code % 4096], tiles[t - start], preferred_element_type=F32)
            sums.append((jnp.where(t < end, (code // 4096) % spare, spare), total))
        for rb, total in sums:
            acc[rb] += total
        return carry

    lax.fori_loop(0, (end - begin + APPLY_UNROLL - 1) // APPLY_UNROLL, some, 0)


def far_kernel(nz, ny, nb, *refs):
    geos, pays, refs = refs[:nz], refs[nz : nz + ny], refs[nz + ny :]
    outs, refs = refs[: nz - 1], refs[nz - 1 :]
    tiles, pairs, features, own = refs[0], refs[1], refs[2:7], refs[7:]
    acc = own[0]
    _, bounds = sections(nz, ny)
    prepare(nz, ny, nb, geos, pays, None, pairs, features, *own)
    form_and_apply(0, pairs[bounds + 2 * nz - 1], 8, nz * nb - 1, pairs, features, tiles, acc)
    put_out(nb, acc, outs, 1)


def near_kernel(nz, ny, nb, pairs, *refs):
    features, out, tiles, acc = refs[:5], refs[5], refs[6], refs[7]
    second, bounds = sections(nz, ny)
    acc[...] = jnp.zeros(acc.shape, F32)
    form_and_apply(second, pairs[bounds + 1], 4, nb - 1, pairs, features, tiles, acc)
    put_out(nb, acc, [out], 0)


def apply_kernel(nz, ny, nb, lines, pairs, *refs):
    tiles, refs = refs[: len(lines)], refs[len(lines) :]
    fluxes, outs, flux, acc = refs[:ny], refs[ny:-2], *refs[-2:]
    second, bounds = sections(nz, ny)
    for m in range(ny):
        for b in range(nb):
            flux[m * nb + b] = fluxes[m][:, b * BLK : (b + 1) * BLK]
    for s, tile, out in zip(lines, tiles, outs):
        acc[...] = jnp.zeros(acc.shape, F32)
        start = 0 if s else second
        apply_tiles(start, pairs[bounds + 2 * s], pairs[bounds + 2 * s + 1], nb, pairs, tile, flux, acc)
        put_out(nb, acc, [out], 0)


def whole_kernel(nz, ny, nb, fresh, *refs):
    geos, pays, refs = refs[:nz], refs[nz : nz + ny], refs[nz + ny :]
    fluxes, refs = (refs[:ny], refs[ny:]) if fresh else (None, refs)
    outs, features, own, pairs = refs[:nz], refs[nz : nz + 5], refs[nz + 5 : -1], refs[-1]
    acc, flux = own[0], features[4]
    _, bounds = sections(nz, ny)
    prepare(nz, ny, nb, geos, pays, fluxes, pairs, features, *own)
    for s in range(nz):

        def one(t, carry):
            code = pairs[t]
            tile = tile_of(code, nz * nb - 1, features)
            acc[code // 4096] += jnp.dot(flux[code % 4096], tile, preferred_element_type=F32)
            return carry

        lax.fori_loop(pairs[bounds + 2 * s], pairs[bounds + 2 * s + 1], one, 0)
    put_out(nb, acc, outs, 0)


def per_device(nz, ny, positions, normals, emission, material, area_level, reflect_table, area_table, pair_slots):
    patches = positions.shape[1]
    nb = patches // BLK
    second, bounds = sections(nz, ny)
    keep = bounds * BLK * BLK * 2 <= KEEP_BYTES

    def call(kernel, name, megabytes, ins, outs, scratch, args):
        spaces = [SMEM() if getattr(x, "memory_space", None) == pltpu.SMEM else VMEM() for x in outs]
        return pl.pallas_call(
            kernel,
            out_shape=tuple(outs),
            in_specs=ins,
            out_specs=tuple(spaces),
            scratch_shapes=scratch,
            compiler_params=megabytes and pltpu.CompilerParams(vmem_limit_bytes=megabytes * 2**20),
            name=name,
        )(*args)

    payload, geo, area, reflect, emission = call(
        pack_kernel,
        "pack",
        None,
        [VMEM()] * 8,
        [
            pltpu.VMEM((GEO + BANDS, patches), BF16),
            pltpu.VMEM((GEO, patches), BF16),
            pltpu.VMEM((1, patches), F32),
            pltpu.VMEM((BANDS, patches), F32),
            pltpu.VMEM((BANDS, patches), F32),
        ],
        [pltpu.VMEM((GEO, patches), F32)],
        (
            positions,
            normals,
            emission,
            area_level.reshape(1, patches),
            area_table.reshape(1, -1),
            material.reshape(1, patches),
            reflect_table,
            jnp.transpose(pair_slots[0], (1, 2, 0)),
        ),
    )

    def exchange(row_source, column_source, after):
        got = {"z0": row_source, "m0": column_source}
        todo = [] if row_source is None else [f"z{s}" for s in range(1, nz)]
        todo += [f"m{m}" for m in range(2, ny, 2)] + [f"m{m}" for m in range(1, ny, 2)]
        while todo:
            for name in list(todo):
                far, step = name[0] == "z", int(name[1:])
                source = "z0" if far else f"m{step - 1}" if step % 2 else "m0"
                if source not in got or after.get(name, source) not in got:
                    continue
                held = got[source]
                if name in after:
                    held, _ = lax.optimization_barrier((held, got[after[name]]))
                if far:
                    got[name] = lax.ppermute(held, "gx", [(i, (i + step) % nz) for i in range(nz)])
                else:
                    turn = 1 if step % 2 else step
                    got[name] = lax.ppermute(held, "gy", [(i, i ^ turn) for i in range(ny)])
                todo.remove(name)
        return got

    def sent(parts):
        return [
            lax.ppermute(part, "gx", [(i, (i - s) % nz) for i in range(nz)])
            for s, part in enumerate(parts, 1)
        ]

    def total(own, parts):
        for part in parts:
            own = own + part.astype(F32)
        return own

    own_part = jax.ShapeDtypeStruct((BANDS, patches), F32)
    far_parts = [jax.ShapeDtypeStruct((BANDS, patches), BF16)] * (nz - 1)
    features, own = feature_scratch(nz, ny, nb), own_scratch(nz, ny, nb)
    acc = own[0]
    pairs_list = pltpu.SMEM((bounds + 2 * nz,), jnp.int32)

    ordered = nz == 4 and ny == 8
    got = exchange(geo, payload, FIRST_ORDER if ordered else {})
    rows, cols = [got[f"z{s}"] for s in range(nz)], [got[f"m{m}"] for m in range(ny)]

    def whole(fluxes):
        got = call(
            functools.partial(whole_kernel, nz, ny, nb, bool(fluxes)),
            "whole",
            60,
            [VMEM()] * (nz + ny + len(fluxes)),
            [own_part] + far_parts,
            features + own + [pairs_list],
            (*rows, *cols, *fluxes),
        )
        return total(got[0], sent(got[1:]))

    if keep:
        got = call(
            functools.partial(far_kernel, nz, ny, nb),
            "far",
            16,
            [VMEM()] * (nz + ny),
            far_parts + [pltpu.VMEM((second, BLK, BLK), BF16), pairs_list] + features,
            own,
            (*rows, *cols),
        )
        returned = sent(got[: nz - 1])
        far_tiles, pairs, *kept = got[nz - 1 :]
        own_sum, near_tiles = call(
            functools.partial(near_kernel, nz, ny, nb),
            "near",
            8,
            [SMEM()] + [VMEM()] * 5,
            [own_part, pltpu.VMEM((bounds - second, BLK, BLK), BF16)],
            [pltpu.VMEM((nb + 1, BANDS, BLK), F32)],
            (pairs, *kept),
        )
        irradiation = total(own_sum, returned)
    else:
        irradiation = whole([])
    radiosity = emission + reflect * irradiation
    got = exchange(None, (area * radiosity).astype(BF16), LATER_ORDER if ordered else {})
    fluxes = [got[f"m{m}"] for m in range(ny)]
    if keep:
        parts = {}
        for lines in TOGETHER if ordered else [range(1, nz), [0]]:
            got = call(
                functools.partial(apply_kernel, nz, ny, nb, lines),
                "apply",
                4,
                [SMEM()] + [VMEM()] * (len(lines) + ny),
                [far_parts[0] if s else own_part for s in lines],
                [features[4], pltpu.VMEM((nb + 1, BANDS, BLK), F32)],
                (pairs, *[far_tiles if s else near_tiles for s in lines], *fluxes),
            )
            parts.update(zip(lines, got))
        irradiation = total(parts[0], sent([parts[s] for s in range(1, nz)]))
    else:
        irradiation = whole(fluxes)
    return emission + reflect * irradiation


def solution(mesh):
    nz, ny = mesh.shape["gx"], mesh.shape["gy"]
    both = ("gx", "gy")
    placed = (
        P(None, both),
        P(None, both),
        P(None, both),
        P(both),
        P(both),
        P(),
        P(),
        P(both, None, None, None),
    )
    return jax.shard_map(
        functools.partial(per_device, nz, ny),
        mesh=mesh,
        in_specs=placed,
        out_specs=P(None, both),
        check_vma=False,
    )
```

```python
import functools
import math

import jax
import jax.numpy as jnp
from jax import lax
from jax.experimental import pallas as pl
from jax.experimental.pallas import tpu as pltpu
from jax.sharding import PartitionSpec as P

BANDS = 16
BLK = 256
CAP = 2
GEO = 16
LANES = 128
KDIM = 48
APPLY_UNROLL = 8
SPARE = 8
FIRST_ORDER = {"m1": "z1", "m3": "z2", "m5": "z3"}
LATER_ORDER = {}
TOGETHER = [(1,), (2,), (3,), (0,)]
KEEP_BYTES = 24 * 2**20
BF16 = jnp.bfloat16
F32 = jnp.float32

VMEM = functools.partial(pl.BlockSpec, memory_space=pltpu.VMEM)
SMEM = functools.partial(pl.BlockSpec, memory_space=pltpu.SMEM)


def split(value, terms):
    out = []
    for _ in range(terms):
        part = value.astype(BF16).astype(F32)
        out.append(part)
        value = value - part
    return out


def pack_kernel(
    pos_ref, nrm_ref, emi_ref, level_ref, table_ref, kind_ref, share_ref, slot_ref, pay_ref, geo_ref, area_ref, reflect_ref, kept_ref, rows
):
    level = level_ref[...]
    area = jnp.zeros(level.shape, F32)
    for k in range(table_ref.shape[1]):
        area = jnp.where(level == k, table_ref[:, k : k + 1], area)
    area_ref[...] = area
    p1, p2 = split(pos_ref[...], 2)
    n1, n2 = split(nrm_ref[...], 2)
    a1, a2 = split(area, 2)
    rows[0:3, :] = p1
    rows[3:6, :] = p2
    rows[6:7, :] = a1
    rows[7:8, :] = a2
    rows[8:11, :] = n1
    rows[11:14, :] = n2
    rows[14:16, :] = jnp.zeros((2, area.shape[1]), F32)
    peers = slot_ref.shape[-1]
    for t in range(2 * CAP):
        rows[14:15, t * LANES : t * LANES + peers] = slot_ref[t // 2, t % 2 : t % 2 + 1, :].astype(F32)
    geo = rows[...].astype(BF16)
    geo_ref[...] = geo
    pay_ref[0:GEO, :] = geo
    pay_ref[GEO:, :] = (area * emi_ref[...]).astype(BF16)
    kind = jnp.broadcast_to(kind_ref[...], reflect_ref.shape)
    share = jnp.transpose(share_ref[...])
    reflect = jnp.zeros(reflect_ref.shape, F32)
    for k in range(share.shape[1]):
        reflect = jnp.where(kind == k, share[:, k : k + 1], reflect)
    reflect_ref[...] = reflect
    kept_ref[...] = emi_ref[...]


def terms_of(g):
    pos, nrm = g[0:8], g[8:16]
    row = lax.broadcasted_iota(jnp.int32, pos.shape, 0)
    p = pos + pltpu.roll(pos, 5, 0)
    n = nrm + pltpu.roll(nrm, 5, 0)
    half = 0.5 * (pos[6:7] + pos[7:8])
    pp = jnp.sum(jnp.where(row < 3, p * p, 0.0), axis=0, keepdims=True)
    dot = jnp.sum(jnp.where(row < 3, n * p, 0.0), axis=0, keepdims=True)
    area = (1.0 - 1.0 / math.pi) * half
    terms = split(jnp.where(row == 0, pp + half, jnp.where(row == 1, -dot, area)), 3)
    return pos, nrm, row, terms, area


def column_features(g):
    pos, nrm, row, terms, _ = terms_of(g)
    zero = jnp.zeros(pos.shape, F32)
    one = jnp.where(row == 6, 1.0, zero)
    pos = jnp.where(row < 6, pos, one)
    nrm = jnp.where(row < 6, nrm, one)
    later = jnp.where(row < 6, pltpu.roll(terms[1], 3, 0), pltpu.roll(terms[2], 6, 0))
    consts = jnp.where(row < 3, terms[0], later)
    return jnp.concatenate([pos, nrm, pos, nrm, consts, zero], axis=0)


def row_features(g):
    pos, nrm, row, terms, area = terms_of(g)
    zero = jnp.zeros(pos.shape, F32)

    def both(x):
        high = jnp.where(row < 3, x, pltpu.roll(x, 3, 0))
        low = jnp.where(row < 3, pltpu.roll(x, 5, 0), x)
        return jnp.where(row < 6, high, 0.0), jnp.where(row < 6, low, 0.0)

    def with_last(x, t, which):
        return jnp.where(row == 6, terms[t][which : which + 1], x)

    def ones(first):
        return jnp.where(row % 3 == first, 1.0, zero)

    p_hi, p_lo = both(pos)
    n_hi, n_lo = both(nrm)
    facing = [with_last(n_hi, 0, 1), with_last(zero, 1, 1), with_last(n_lo, 2, 1), zero, zero, zero]
    seen = [zero, p_hi, zero, p_lo, ones(1), zero]
    near = [
        with_last(-2.0 * p_hi, 0, 0),
        with_last(zero, 1, 0),
        with_last(-2.0 * p_lo, 2, 0),
        zero,
        ones(0),
        zero,
    ]
    return [jnp.concatenate(parts, axis=0).astype(BF16) for parts in (facing, seen, near)], area


def sections(nz, ny):
    one = ny * 2 * CAP
    second = (nz - 1) * one + 2 * SPARE
    return second, second + one + 2 * SPARE


def list_pairs(nz, ny, nb, slots, pairs):
    z, k = lax.axis_index("gx"), lax.axis_index("gy")
    second, bounds = sections(nz, ny)

    def peer(s, m, count):
        zs = lax.rem(z - s + nz, nz)
        own = z * ny + jnp.bitwise_xor(k, m)
        served = zs * ny + k
        for t in range(CAP):
            row, col = slots[s, 2 * t * LANES + own], slots[s, (2 * t + 1) * LANES + own]
            pairs[count] = (s * nb + row) * 4096 + m * nb + col
            count = count + (row >= 0).astype(jnp.int32)
            col, row = slots[nz + m, 2 * t * LANES + served], slots[nz + m, (2 * t + 1) * LANES + served]
            pairs[count] = (s * nb + row) * 4096 + m * nb + col
            count = count + (row >= 0).astype(jnp.int32)
        return count

    for start, lines in ((0, range(1, nz)), (second, range(1))):
        for t in range(SPARE):
            pairs[start + t] = nz * nb * 4096
        count = jnp.int32(start + SPARE)
        for s in lines:
            pairs[bounds + 2 * s] = count
            if ny <= 8:
                for m in range(ny):
                    count = peer(s, m, count)
            else:
                count = lax.fori_loop(0, ny, functools.partial(peer, s), count)
            pairs[bounds + 2 * s + 1] = count
        for t in range(SPARE):
            pairs[count + t] = nz * nb * 4096


def feature_scratch(nz, ny, nb):
    return [
        pltpu.VMEM((nz * nb, 3, KDIM, BLK), BF16),
        pltpu.VMEM((nz * nb, 1, BLK), F32),
        pltpu.VMEM((ny * nb, BLK, KDIM), BF16),
        pltpu.VMEM((ny * nb, BLK, LANES), F32),
        pltpu.VMEM((ny * nb, BANDS, BLK), BF16),
    ]


def own_scratch(nz, ny, nb):
    devices = -(-(nz + ny) // 8) * 8
    return [
        pltpu.VMEM((nz * nb + 1, BANDS, BLK), F32),
        pltpu.VMEM((devices, 2 * CAP * LANES), jnp.int32),
        pltpu.SMEM((devices, 2 * CAP * LANES), jnp.int32),
        pltpu.SemaphoreType.DMA,
    ]


def put_out(nb, acc, out_refs, first):
    for s, out in enumerate(out_refs):
        for b in range(nb):
            out[:, b * BLK : (b + 1) * BLK] = (acc[(first + s) * nb + b] * (1.0 / math.pi)).astype(out.dtype)


def prepare(nz, ny, nb, geos, pays, fluxes, pairs, features, acc, slots_v, slots, sem):
    row_feat, row_area, col_feat, col_area, flux = features
    width = slots.shape[1]
    for s in range(nz):
        g = geos[s][...].astype(F32)
        slots_v[s : s + 1, :] = g[14:15, :width].astype(jnp.int32)
    for m in range(ny):
        g = pays[m][0:GEO, :].astype(F32)
        slots_v[nz + m : nz + m + 1, :] = g[14:15, :width].astype(jnp.int32)
    copy = pltpu.make_async_copy(slots_v, slots, sem)
    copy.start()
    for s in range(nz):
        forms, h = row_features(geos[s][...].astype(F32))
        for b in range(nb):
            here = slice(b * BLK, (b + 1) * BLK)
            row_area[s * nb + b] = h[:, here]
            for v in range(3):
                row_feat[s * nb + b, v] = forms[v][:, here]
    acc[...] = jnp.zeros(acc.shape, F32)
    copy.wait()
    list_pairs(nz, ny, nb, slots, pairs)
    depth = lax.broadcasted_iota(jnp.int32, (KDIM, LANES), 0)
    pick = jnp.where((depth == 34) | (depth == 37), 1.0, 0.0).astype(BF16)
    for m in range(ny):
        feat = column_features(pays[m][0:GEO, :].astype(F32)).astype(BF16)
        for b in range(nb):
            here = slice(b * BLK, (b + 1) * BLK)
            turned = jnp.transpose(feat[:, here])
            col_feat[m * nb + b] = turned
            col_area[m * nb + b] = jnp.dot(turned, pick, preferred_element_type=F32)
            flux[m * nb + b] = fluxes[m][:, here] if fluxes else pays[m][GEO:, here]


def tile_of(code, last, features):
    row_feat, row_area, col_feat, col_area, _ = features
    rb, cb = jnp.minimum(code // 4096, last), code % 4096
    left = col_feat[cb]
    f, s, q = (jnp.dot(left, row_feat[rb, v], preferred_element_type=F32) for v in range(3))
    area = col_area[cb]
    area = jnp.concatenate([area] * (BLK // LANES), axis=1) + row_area[rb]
    top = jnp.maximum(f, 0.0) * jnp.maximum(s, 0.0)
    return (top * pltpu.reciprocal(q * (q - area), approx=True)).astype(BF16)


def form_and_apply(start, end, unroll, last, pairs, features, tiles, acc):
    flux = features[4]

    def add(step):
        sums = []
        for u in range(unroll):
            t = step * unroll + u
            code = pairs[start + t]
            total = jnp.dot(flux[code % 4096], tiles[t], preferred_element_type=F32)
            sums.append((jnp.minimum(code // 4096, last + 1), total))
        return sums

    def some(step, carry):
        sums = add(step - 1)
        for u in range(unroll):
            t = step * unroll + u
            tiles[t] = tile_of(pairs[start + t], last, features)
        for rb, total in sums:
            acc[rb] += total
        return carry

    first = SPARE // unroll
    steps = (end - start + unroll - 1) // unroll
    lax.fori_loop(first, steps, some, 0)
    for rb, total in add(steps - 1):
        acc[rb] += total


def apply_tiles(start, begin, end, spare, pairs, tiles, flux, acc):
    def some(step, carry):
        sums = []
        for u in range(APPLY_UNROLL):
            t = begin + step * APPLY_UNROLL + u
            code = pairs[t]
            total = jnp.dot(flux[code % 4096], tiles[t - start], preferred_element_type=F32)
            sums.append((jnp.where(t < end, (code // 4096) % spare, spare), total))
        for rb, total in sums:
            acc[rb] += total
        return carry

    lax.fori_loop(0, (end - begin + APPLY_UNROLL - 1) // APPLY_UNROLL, some, 0)


def far_kernel(nz, ny, nb, *refs):
    geos, pays, refs = refs[:nz], refs[nz : nz + ny], refs[nz + ny :]
    outs, refs = refs[: nz - 1], refs[nz - 1 :]
    tiles, pairs, features, own = refs[0], refs[1], refs[2:7], refs[7:]
    acc = own[0]
    _, bounds = sections(nz, ny)
    prepare(nz, ny, nb, geos, pays, None, pairs, features, *own)
    form_and_apply(0, pairs[bounds + 2 * nz - 1], 8, nz * nb - 1, pairs, features, tiles, acc)
    put_out(nb, acc, outs, 1)


def near_kernel(nz, ny, nb, pairs, *refs):
    features, out, tiles, acc = refs[:5], refs[5], refs[6], refs[7]
    second, bounds = sections(nz, ny)
    acc[...] = jnp.zeros(acc.shape, F32)
    form_and_apply(second, pairs[bounds + 1], 4, nb - 1, pairs, features, tiles, acc)
    put_out(nb, acc, [out], 0)


def apply_kernel(nz, ny, nb, lines, laid, pairs, *refs):
    tiles, refs = refs[: len(lines)], refs[len(lines) :]
    acc = refs[-1]
    second, bounds = sections(nz, ny)
    if laid:
        flux, outs = refs[0], refs[1:-1]
    else:
        fluxes, outs, flux = refs[:ny], refs[ny:-2], refs[-2]
        for m in range(ny):
            for b in range(nb):
                flux[m * nb + b] = fluxes[m][:, b * BLK : (b + 1) * BLK]
    for s, tile, out in zip(lines, tiles, outs):
        acc[...] = jnp.zeros(acc.shape, F32)
        start = 0 if s else second
        apply_tiles(start, pairs[bounds + 2 * s], pairs[bounds + 2 * s + 1], nb, pairs, tile, flux, acc)
        put_out(nb, acc, [out], 0)


def whole_kernel(nz, ny, nb, fresh, *refs):
    geos, pays, refs = refs[:nz], refs[nz : nz + ny], refs[nz + ny :]
    fluxes, refs = (refs[:ny], refs[ny:]) if fresh else (None, refs)
    outs, features, own, pairs = refs[:nz], refs[nz : nz + 5], refs[nz + 5 : -1], refs[-1]
    acc, flux = own[0], features[4]
    _, bounds = sections(nz, ny)
    prepare(nz, ny, nb, geos, pays, fluxes, pairs, features, *own)
    for s in range(nz):

        def one(t, carry):
            code = pairs[t]
            tile = tile_of(code, nz * nb - 1, features)
            acc[code // 4096] += jnp.dot(flux[code % 4096], tile, preferred_element_type=F32)
            return carry

        lax.fori_loop(pairs[bounds + 2 * s], pairs[bounds + 2 * s + 1], one, 0)
    put_out(nb, acc, outs, 0)


def per_device(nz, ny, positions, normals, emission, material, area_level, reflect_table, area_table, pair_slots):
    patches = positions.shape[1]
    nb = patches // BLK
    second, bounds = sections(nz, ny)
    keep = bounds * BLK * BLK * 2 <= KEEP_BYTES

    def call(kernel, name, megabytes, ins, outs, scratch, args):
        spaces = [SMEM() if getattr(x, "memory_space", None) == pltpu.SMEM else VMEM() for x in outs]
        return pl.pallas_call(
            kernel,
            out_shape=tuple(outs),
            in_specs=ins,
            out_specs=tuple(spaces),
            scratch_shapes=scratch,
            compiler_params=megabytes and pltpu.CompilerParams(vmem_limit_bytes=megabytes * 2**20),
            name=name,
        )(*args)

    payload, geo, area, reflect, emission = call(
        pack_kernel,
        "pack",
        None,
        [VMEM()] * 8,
        [
            pltpu.VMEM((GEO + BANDS, patches), BF16),
            pltpu.VMEM((GEO, patches), BF16),
            pltpu.VMEM((1, patches), F32),
            pltpu.VMEM((BANDS, patches), F32),
            pltpu.VMEM((BANDS, patches), F32),
        ],
        [pltpu.VMEM((GEO, patches), F32)],
        (
            positions,
            normals,
            emission,
            area_level.reshape(1, patches),
            area_table.reshape(1, -1),
            material.reshape(1, patches),
            reflect_table,
            jnp.transpose(pair_slots[0], (1, 2, 0)),
        ),
    )

    def exchange(row_source, column_source, after):
        got = {"z0": row_source, "m0": column_source}
        todo = [] if row_source is None else [f"z{s}" for s in range(1, nz)]
        todo += [f"m{m}" for m in range(2, ny, 2)] + [f"m{m}" for m in range(1, ny, 2)]
        while todo:
            for name in list(todo):
                far, step = name[0] == "z", int(name[1:])
                source = "z0" if far else f"m{step - 1}" if step % 2 else "m0"
                if source not in got or after.get(name, source) not in got:
                    continue
                held = got[source]
                if name in after:
                    held, _ = lax.optimization_barrier((held, got[after[name]]))
                if far:
                    got[name] = lax.ppermute(held, "gx", [(i, (i + step) % nz) for i in range(nz)])
                else:
                    turn = 1 if step % 2 else step
                    got[name] = lax.ppermute(held, "gy", [(i, i ^ turn) for i in range(ny)])
                todo.remove(name)
        return got

    def sent(parts):
        return [
            lax.ppermute(part, "gx", [(i, (i - s) % nz) for i in range(nz)])
            for s, part in enumerate(parts, 1)
        ]

    def total(own, parts):
        for part in parts:
            own = own + part.astype(F32)
        return own

    own_part = jax.ShapeDtypeStruct((BANDS, patches), F32)
    far_parts = [jax.ShapeDtypeStruct((BANDS, patches), BF16)] * (nz - 1)
    features, own = feature_scratch(nz, ny, nb), own_scratch(nz, ny, nb)
    acc = own[0]
    pairs_list = pltpu.SMEM((bounds + 2 * nz,), jnp.int32)

    ordered = nz == 4 and ny == 8
    got = exchange(geo, payload, FIRST_ORDER if ordered else {})
    rows, cols = [got[f"z{s}"] for s in range(nz)], [got[f"m{m}"] for m in range(ny)]

    def whole(fluxes):
        got = call(
            functools.partial(whole_kernel, nz, ny, nb, bool(fluxes)),
            "whole",
            60,
            [VMEM()] * (nz + ny + len(fluxes)),
            [own_part] + far_parts,
            features + own + [pairs_list],
            (*rows, *cols, *fluxes),
        )
        return total(got[0], sent(got[1:]))

    if keep:
        got = call(
            functools.partial(far_kernel, nz, ny, nb),
            "far",
            16,
            [VMEM()] * (nz + ny),
            far_parts + [pltpu.VMEM((second, BLK, BLK), BF16), pairs_list] + features,
            own,
            (*rows, *cols),
        )
        returned = sent(got[: nz - 1])
        far_tiles, pairs, *kept = got[nz - 1 :]
        own_sum, near_tiles = call(
            functools.partial(near_kernel, nz, ny, nb),
            "near",
            8,
            [SMEM()] + [VMEM()] * 5,
            [own_part, pltpu.VMEM((bounds - second, BLK, BLK), BF16)],
            [pltpu.VMEM((nb + 1, BANDS, BLK), F32)],
            (pairs, *kept),
        )
        irradiation = total(own_sum, returned)
    else:
        irradiation = whole([])
    radiosity = emission + reflect * irradiation
    got = exchange(None, (area * radiosity).astype(BF16), LATER_ORDER if ordered else {})
    fluxes = [got[f"m{m}"] for m in range(ny)]
    if keep:
        parts, flux = {}, None
        for lines in TOGETHER if ordered else [range(1, nz), [0]]:
            got = call(
                functools.partial(apply_kernel, nz, ny, nb, lines, flux is not None),
                "apply",
                4,
                [SMEM()] + [VMEM()] * (len(lines) + (ny if flux is None else 1)),
                [far_parts[0] if s else own_part for s in lines] + ([features[4]] if flux is None else []),
                [pltpu.VMEM((nb + 1, BANDS, BLK), F32)],
                (pairs, *[far_tiles if s else near_tiles for s in lines], *(fluxes if flux is None else [flux])),
            )
            flux = got[-1] if flux is None else flux
            parts.update(zip(lines, got))
        irradiation = total(parts[0], sent([parts[s] for s in range(1, nz)]))
    else:
        irradiation = whole(fluxes)
    return emission + reflect * irradiation


def solution(mesh):
    nz, ny = mesh.shape["gx"], mesh.shape["gy"]
    both = ("gx", "gy")
    placed = (
        P(None, both),
        P(None, both),
        P(None, both),
        P(both),
        P(both),
        P(),
        P(),
        P(both, None, None, None),
    )
    return jax.shard_map(
        functools.partial(per_device, nz, ny),
        mesh=mesh,
        in_specs=placed,
        out_specs=P(None, both),
        check_vma=False,
    )
```
